512 devices in a mesh: dp: 32 (over y, z_lo, core), group: 16 (over z_hi, x).
Axes of the slice: x: 4, y: 8, z: 8 (z_hi: 4, z_lo: 2; z = z_hi * 2 + z_lo), core: 2. Of those that a mesh axis runs over, the one named last changes fastest.
Arguments:
- glu_in: bfloat16 [131072, 3072], P(('dp', 'group'))
- cotangent: bfloat16 [131072, 1536], P(('dp', 'group')), may hold values from -6 to 6
- frame_count: int32 [1024], P(('dp', 'group')), may hold values from 64 to 128, as said below
- kernel: bfloat16 [16, 32, 1536], P('group'), may hold values from -1 to 1
- norm_params: bfloat16 [16, 2, 1536], P('group'), may hold values from 0.5 to 1.5
- drift_kernel: bfloat16 [16, 32, 1536], P('group'), may hold values from -8 to 8
- drift_norm: bfloat16 [16, 2, 1536], P('group'), may hold values from -8 to 8
Outputs:
- kernel_average: float32 [32, 1536], P(None, 'dp')
- norm_average: float32 [2, 1536], P(None, 'dp')
The draws below stay inside these ranges and needn't reach their ends.
Inputs may be any that keep to these rules, and one draw needn't show every extreme that they name: `frame_count`: frame counts of the utterance slots; some utterance fills all 128 frames.
All inputs are finite; a program needn't handle non-finite values.
Results may differ from the reference program's by a relative error of at most 0.007.
Values sent between devices are 32-bit elements; how exact they have to be, the bound alone decides.
No kernel may reach another device: no remote copies, remote signals or barrier semaphores. Data moves between devices by JAX's collectives and lax.ppermute only.
A program may use at most 64 MiB of HBM per device.

```python
import math
import jax
import jax.numpy as jnp
from jax import lax

D = 1536
K = 32
SLOT = 128
UTT_DEV = 2
ROWS = 256
TOTAL_ROWS = 131072
N_DP = 32
N_GROUP = 16


def draw_frame_count(key, part):
    key = jax.random.fold_in(key, 11)
    count_all = N_DP * N_GROUP * UTT_DEV
    position = jnp.arange(count_all, dtype=jnp.int32)
    group_of = position // UTT_DEV % N_GROUP
    floor_len = SLOT // 2
    ceiling = floor_len + (SLOT - floor_len) * (group_of + 1) // N_GROUP
    lengths = jax.random.randint(key, (count_all,), floor_len, ceiling + 1)
    lengths = jnp.where(position == (N_GROUP - 1) * UTT_DEV, SLOT, lengths)
    return lengths.astype(jnp.int32)


def draw_glu_in(key, part):
    key = jax.random.fold_in(key, 23)
    keys_all = jax.random.split(key, 4)
    row_total = ROWS * N_DP * N_GROUP
    device_dp = jnp.arange(row_total) // ROWS // N_GROUP
    rising = 1.0 + 2.0 * device_dp.astype(jnp.float32) / float(max(N_DP - 1, 1))
    channel_scale = jnp.exp(jax.random.uniform(keys_all[0], (1, 2 * D), jnp.float32, math.log(0.3), math.log(3.0)))
    noise = jax.random.normal(keys_all[1], (row_total, 2 * D), jnp.float32)
    row_scale = jnp.exp(jax.random.uniform(keys_all[2], (row_total, 1), jnp.float32, math.log(0.5), math.log(2.0)))
    offset = 0.5 * jax.random.normal(keys_all[3], (1, 2 * D), jnp.float32)
    field = (noise * channel_scale + offset) * row_scale * rising[:, None]
    return field.astype(jnp.bfloat16)


def level_of(key, dims, pieces, least, high):
    factor_of = 1.0
    for axis_at, shards_of in pieces:
        steps = jax.random.uniform(jax.random.fold_in(jax.random.fold_in(key, 6), axis_at), (shards_of,), jnp.float32, least / len(pieces), high / len(pieces))
        factor_of = factor_of * jnp.repeat(jnp.exp(steps), dims[axis_at] // shards_of).reshape((-1,) + (1,) * (len(dims) - 1 - axis_at))
    return factor_of


def centred(rng, extent, deviation, bound, cuts=(), kind=jnp.bfloat16):
    array = deviation * jax.random.normal(rng, extent, jnp.float32)
    if cuts:
        array = array * level_of(rng, extent, cuts, -0.22, 0.18)
    return jnp.clip(array, -bound, bound).astype(kind)


def setup_inputs(seed: int = 0) -> dict:
    key_list = jax.random.split(jax.random.key(seed), 8)
    glu_in = draw_glu_in(jax.random.fold_in(key_list[7], 71), 0)
    cotangent = centred(key_list[1], (TOTAL_ROWS, D), 1.0, 6.0, ((0, 512),))
    frame_count = draw_frame_count(jax.random.fold_in(key_list[7], 71), 0)
    kernel = centred(key_list[3], (N_GROUP, K, D), K ** -0.5, 1.0, ((0, 16),))
    norm_params = jnp.clip(0.5 + 1.0 * jax.random.uniform(key_list[4], (N_GROUP, 2, D), jnp.float32) ** level_of(key_list[4], (N_GROUP, 2, D), ((0, 16),), -0.2, 0.2), 0.5, 1.5).astype(jnp.bfloat16)
    drift_kernel = centred(key_list[5], (N_GROUP, K, D), 1.5, 8.0, ((0, 16),))
    drift_norm = centred(key_list[6], (N_GROUP, 2, D), 1.5, 8.0, ((0, 16),))
    return dict(glu_in=glu_in, cotangent=cotangent, frame_count=frame_count, kernel=kernel, norm_params=norm_params, drift_kernel=drift_kernel, drift_norm=drift_norm)


grad_factor_base = 128.0
eps_norm = 1e-05

def gated_input(inputs, counts):
    utterances = counts.shape[0]
    channels = inputs.shape[1] // 2
    slot_len = inputs.shape[0] // utterances
    position = lax.broadcasted_iota(jnp.int32, (utterances, slot_len), 1)
    live_mask = (position < counts[:, None]).astype(jnp.float32)[:, :, None]
    values = inputs[:, :channels].astype(jnp.float32).reshape(utterances, slot_len, channels)
    gate_part = inputs[:, channels:].astype(jnp.float32).reshape(utterances, slot_len, channels)
    return (values * jax.nn.sigmoid(gate_part) * live_mask, live_mask)

def pad_field(gated_field):
    left_pad = K // 2
    return jnp.pad(gated_field, ((0, 0), (left_pad, K - 1 - left_pad), (0, 0)))

def depthwise(padded, kernel_f, slot_len):
    summed = padded[:, 0:slot_len, :] * kernel_f[0]
    for tap_index in range(1, K):
        summed = summed + padded[:, tap_index:tap_index + slot_len, :] * kernel_f[tap_index]
    return summed

def kernel_terms(padded, conv_back, slot_len):
    return jnp.stack([lax.optimization_barrier(jnp.sum(padded[:, tap_index:tap_index + slot_len, :] * conv_back, axis=(0, 1))) for tap_index in range(K)])

def reference(glu_in, cotangent, frame_count, kernel, norm_params, drift_kernel, drift_norm):
    by_group = glu_in.reshape(N_DP, N_GROUP, UTT_DEV * SLOT, 2 * D)
    cot_group = cotangent.reshape(N_DP, N_GROUP, UTT_DEV * SLOT, D)
    count_group = frame_count.reshape(N_DP, N_GROUP, UTT_DEV)

    def one_group(group_id):
        inputs = lax.dynamic_index_in_dim(by_group, group_id, 1, False).reshape(N_DP * UTT_DEV * SLOT, 2 * D)
        cot_rows = lax.dynamic_index_in_dim(cot_group, group_id, 1, False).reshape(N_DP * UTT_DEV, SLOT, D)
        counts = lax.dynamic_index_in_dim(count_group, group_id, 1, False).reshape(N_DP * UTT_DEV)
        kernel_f = lax.dynamic_index_in_dim(kernel, group_id, 0, False).astype(jnp.float32)
        params_f = lax.dynamic_index_in_dim(norm_params, group_id, 0, False).astype(jnp.float32)
        drift_k = lax.dynamic_index_in_dim(drift_kernel, group_id, 0, False).astype(jnp.float32)
        drift_n = lax.dynamic_index_in_dim(drift_norm, group_id, 0, False).astype(jnp.float32)
        gated_field, live_mask = gated_input(inputs, counts)
        padded = pad_field(gated_field)
        conv_out = depthwise(padded, kernel_f, SLOT)
        frames = jnp.sum(counts).astype(jnp.float32)
        mean_value = lax.optimization_barrier(jnp.sum(conv_out * live_mask, axis=(0, 1))) / frames
        centered = (conv_out - mean_value) * live_mask
        variance = lax.optimization_barrier(jnp.sum(centered * centered, axis=(0, 1))) / frames
        inverse = lax.rsqrt(variance + eps_norm)
        normed = (conv_out - mean_value) * inverse
        norm_gain = params_f[0]
        norm_shift = params_f[1]
        norm_out = norm_gain * normed + norm_shift
        sigmoid_out = jax.nn.sigmoid(norm_out)
        swish_slope = sigmoid_out * (1.0 + norm_out * (1.0 - sigmoid_out))
        upstream = cot_rows.astype(jnp.float32) * live_mask * swish_slope
        norm_sums = jnp.stack([lax.optimization_barrier(jnp.sum(upstream * normed, axis=(0, 1))), lax.optimization_barrier(jnp.sum(upstream, axis=(0, 1)))])
        conv_back = norm_gain * inverse * (upstream - (norm_sums[1] + normed * norm_sums[0]) / frames) * live_mask
        kernel_sum = kernel_terms(padded, conv_back, SLOT)
        grad_factor = grad_factor_base / frames
        kernel_delta = (drift_k + kernel_sum * grad_factor).astype(jnp.bfloat16)
        norm_delta = (drift_n + norm_sums * grad_factor).astype(jnp.bfloat16)
        kernel_delta = lax.optimization_barrier(kernel_delta)
        norm_delta = lax.optimization_barrier(norm_delta)
        return (kernel_delta.astype(jnp.float32) * frames, norm_delta.astype(jnp.float32) * frames, frames)
    kernel_parts, norm_parts, frame_parts = lax.map(one_group, jnp.arange(N_GROUP, dtype=jnp.int32))
    weight_total = jnp.sum(frame_parts)
    return (lax.optimization_barrier(jnp.sum(kernel_parts, axis=0)) / weight_total, lax.optimization_barrier(jnp.sum(norm_parts, axis=0)) / weight_total)
```

```python
import functools

import jax
import jax.numpy as jnp
from jax import lax
from jax.experimental import pallas as pl
from jax.experimental.pallas import tpu as pltpu
from jax.sharding import PartitionSpec as P

K = 32
HALF = K // 2
SUB = 8
LANES = 128
SLOT = 128
UTT = 2
ROWS = UTT * SLOT
PADDED = HALF + SLOT + HALF
WIDE = SLOT + SUB
STAT_ROWS = 32

grad_factor_base = 128.0
eps_norm = 1e-05


def lane_tile(i):
    return pl.ds(pl.multiple_of(i * LANES, LANES), LANES)


def live_rows(count):
    return lax.broadcasted_iota(jnp.int32, (SLOT, LANES), 0) < count


def conv_kernel(count_ref, glu_ref, kernel_ref, padded_ref, conv_ref, stat_ref, taps_ref):
    channels = conv_ref.shape[1]
    taps_ref[...] = kernel_ref[0].astype(jnp.float32)
    counts = [count_ref[u] for u in range(UTT)]
    local_frames = sum(counts).astype(jnp.float32)
    stat_ref[...] = jnp.full(stat_ref.shape, local_frames, jnp.float32)

    def tile(i, carry):
        lanes = lane_tile(i)
        gate_lanes = lane_tile(i + channels // LANES)
        total = jnp.zeros((SUB, LANES), jnp.float32)
        fields = []
        for u in range(UTT):
            live = live_rows(counts[u])
            rows = pl.ds(u * SLOT, SLOT)
            value = glu_ref[rows, lanes].astype(jnp.float32)
            gate = glu_ref[rows, gate_lanes].astype(jnp.float32)
            base = u * PADDED
            edge = jnp.zeros((HALF, LANES), jnp.float32)
            padded_ref[pl.ds(base, HALF), lanes] = edge
            padded_ref[pl.ds(base + HALF + SLOT, HALF), lanes] = edge
            padded_ref[pl.ds(base + HALF, SLOT), lanes] = jnp.where(
                live, value * jax.nn.sigmoid(gate), 0.0
            )
            summed = None
            for r in range(SUB):
                part = None
                for j in range(K // SUB):
                    tap = taps_ref[pl.ds(r + SUB * j, 1), lanes]
                    term = padded_ref[pl.ds(base + SUB * j, WIDE), lanes] * tap
                    part = term if part is None else part + term
                if r:
                    part = pltpu.roll(part, WIDE - r, 0)
                part = part[:SLOT]
                summed = part if summed is None else summed + part
            conv_ref[rows, lanes] = summed
            masked = jnp.where(live, summed, 0.0)
            total = total + jnp.sum(masked.reshape(SLOT // SUB, SUB, LANES), axis=0)
            fields.append((live, summed))
        local_mean = jnp.sum(total, axis=0, keepdims=True) / local_frames
        spread = jnp.zeros((SUB, LANES), jnp.float32)
        for live, summed in fields:
            centered = jnp.where(live, summed - local_mean, 0.0)
            spread = spread + jnp.sum((centered * centered).reshape(SLOT // SUB, SUB, LANES), axis=0)
        stat_ref[pl.ds(i, 1), :] = local_mean
        stat_ref[pl.ds(i + channels // LANES, 1), :] = jnp.sum(spread, axis=0, keepdims=True)
        return carry

    lax.fori_loop(0, channels // LANES, tile, 0)


def merge_stats(parts, tiles):
    frames = sum(part[2 * tiles : 2 * tiles + 1] for part in parts)
    mean = sum(part[:tiles] * part[2 * tiles : 2 * tiles + 1] for part in parts) / frames
    spread = sum(
        part[tiles : 2 * tiles]
        + part[2 * tiles : 2 * tiles + 1] * (part[:tiles] - mean) * (part[:tiles] - mean)
        for part in parts
    )
    return frames, mean, spread


def pair_kernel(tiles, own_ref, other_ref, out_ref):
    frames, mean, spread = merge_stats([own_ref[...], other_ref[...]], tiles)
    rest = jnp.broadcast_to(frames, (STAT_ROWS - 2 * tiles, LANES))
    for peer in range(out_ref.shape[0]):
        out_ref[peer, pl.ds(0, tiles), :] = mean
        out_ref[peer, pl.ds(tiles, tiles), :] = spread
        out_ref[peer, pl.ds(2 * tiles, STAT_ROWS - 2 * tiles), :] = rest


def back_kernel(
    count_ref, stat_ref, cot_ref, param_ref, padded_ref, conv_ref, out_ref, mean_ref, inv_ref, par_ref, turn_ref
):
    channels = conv_ref.shape[1]
    tiles = channels // LANES
    counts = [count_ref[u] for u in range(UTT)]
    local_frames = sum(counts).astype(jnp.float32)
    frames, mean, spread = merge_stats([stat_ref[p] for p in range(stat_ref.shape[0])], tiles)
    mean_ref[pl.ds(0, tiles), :] = mean
    inv_ref[pl.ds(0, tiles), :] = lax.rsqrt(spread / frames + eps_norm)
    par_ref[...] = param_ref[0].astype(jnp.float32)
    position = lax.broadcasted_iota(jnp.int32, (K, SLOT), 1) + HALF
    position = position - lax.broadcasted_iota(jnp.int32, (K, SLOT), 0)

    def tile(i, carry):
        lanes = lane_tile(i)
        mean_row = mean_ref[pl.ds(i, 1), :]
        inv_row = inv_ref[pl.ds(i, 1), :]
        gain_row = par_ref[pl.ds(0, 1), lanes]
        shift_row = par_ref[pl.ds(1, 1), lanes]
        gain_sum = jnp.zeros((SUB, LANES), jnp.float32)
        shift_sum = jnp.zeros((SUB, LANES), jnp.float32)
        live_sum = jnp.zeros((K, LANES), jnp.float32)
        up_taps = [jnp.zeros((SUB, LANES), jnp.float32) for _ in range(K)]
        norm_taps = [jnp.zeros((SUB, LANES), jnp.float32) for _ in range(K)]
        for u in range(UTT):
            live = live_rows(counts[u])
            rows = pl.ds(u * SLOT, SLOT)
            base = u * PADDED
            normed = (conv_ref[rows, lanes] - mean_row) * inv_row
            norm_out = gain_row * normed + shift_row
            sig = jax.nn.sigmoid(norm_out)
            slope = sig * (1.0 + norm_out * (1.0 - sig))
            upstream = jnp.where(live, cot_ref[rows, lanes].astype(jnp.float32) * slope, 0.0)
            normed = jnp.where(live, normed, 0.0)
            gain_sum = gain_sum + jnp.sum(
                (upstream * normed).reshape(SLOT // SUB, SUB, LANES), axis=0
            )
            shift_sum = shift_sum + jnp.sum(upstream.reshape(SLOT // SUB, SUB, LANES), axis=0)
            edge = jnp.zeros((SUB, LANES), jnp.float32)
            up_wide = jnp.concatenate([upstream, edge], axis=0)
            norm_wide = jnp.concatenate([normed, edge], axis=0)
            for r in range(SUB):
                up_r = pltpu.roll(up_wide, r, 0) if r else up_wide
                norm_r = pltpu.roll(norm_wide, r, 0) if r else norm_wide
                for j in range(K // SUB):
                    k = r + SUB * j
                    field = padded_ref[pl.ds(base + SUB * j, WIDE), lanes]
                    up_taps[k] = up_taps[k] + jnp.sum(
                        (up_r * field).reshape(WIDE // SUB, SUB, LANES), axis=0
                    )
                    norm_taps[k] = norm_taps[k] + jnp.sum(
                        (norm_r * field).reshape(WIDE // SUB, SUB, LANES), axis=0
                    )
            inside = jnp.where((position >= 0) & (position < counts[u]), 1.0, 0.0)
            live_sum = live_sum + jnp.dot(
                inside,
                padded_ref[pl.ds(base + HALF, SLOT), lanes],
                preferred_element_type=jnp.float32,
                precision=lax.Precision.HIGHEST,
            )
        scale = gain_row * inv_row
        up_all = jnp.concatenate([jnp.sum(x, axis=0, keepdims=True) for x in up_taps], axis=0)
        norm_all = jnp.concatenate([jnp.sum(x, axis=0, keepdims=True) for x in norm_taps], axis=0)
        row = lax.broadcasted_iota(jnp.int32, (K, LANES), 0)
        extra = jnp.where(row == 0, jnp.sum(gain_sum, axis=0, keepdims=True), local_frames)
        extra = jnp.where(row == 1, jnp.sum(shift_sum, axis=0, keepdims=True), extra)
        block = jnp.concatenate([up_all * scale, live_sum * scale, norm_all * scale, extra], axis=0)
        turn_ref[lane_tile(i), :] = block.T
        return carry

    lax.fori_loop(0, tiles, tile, 0)
    core = lax.rem(lax.axis_index("dp"), 2)
    chunks = 2 * out_ref.shape[1]
    share = channels // chunks
    for j in range(chunks):
        side = core if j % 2 == 0 else 1 - core
        out_ref[side, j // 2] = turn_ref[pl.ds(j * share, share), :]


def delta_kernel(sum_ref, drift_ref, drift_norm_ref, out_ref):
    share = sum_ref.shape[1]
    channels = drift_ref.shape[2]
    total = sum(sum_ref[p] for p in range(sum_ref.shape[0]))
    frames = total[:, 3 * K + 2 : 3 * K + 3]
    gain_sum = total[:, 3 * K : 3 * K + 1]
    shift_sum = total[:, 3 * K + 1 : 3 * K + 2]
    live_part = pltpu.roll(total, LANES - K, 1)
    norm_part = pltpu.roll(total, LANES - 2 * K, 1)
    kernel_sum = total - (shift_sum * live_part + gain_sum * norm_part) / frames
    start = lax.axis_index("dp") * share
    first = jnp.minimum(start // LANES, channels // LANES - 2)
    window = pl.ds(pl.multiple_of(first * LANES, LANES), 2 * LANES)
    drift = jnp.concatenate(
        [
            drift_ref[0, :, window].astype(jnp.float32),
            drift_norm_ref[0, :, window].astype(jnp.float32),
            jnp.zeros((LANES - K - 2, 2 * LANES), jnp.float32),
        ],
        axis=0,
    )
    drift = pltpu.roll(drift, lax.rem(2 * LANES - (start - first * LANES), 2 * LANES), 1)
    drift = drift[:, :LANES].T[:share]
    lane = lax.broadcasted_iota(jnp.int32, (share, LANES), 1)
    norm_at = pltpu.roll(total, LANES - 2 * K, 1)
    sums = jnp.where(lane < K, kernel_sum, norm_at)
    delta = (drift + (grad_factor_base / frames) * sums).astype(jnp.bfloat16).astype(jnp.float32)
    weighted = delta * frames
    block = share // 3
    lane = lane[:block]
    packed = jnp.broadcast_to(frames[:block], (block, LANES))
    for b in range(3):
        piece = weighted[b * block : (b + 1) * block]
        moved = pltpu.roll(piece, b * K, 1) if b else piece
        packed = jnp.where((lane >= b * K) & (lane < (b + 1) * K), moved, packed)
        at = 3 * K + 2 * b
        moved = pltpu.roll(piece, at - K, 1)
        packed = jnp.where((lane >= at) & (lane < at + 2), moved, packed)
    for peer in range(out_ref.shape[0]):
        out_ref[peer] = packed


def average_kernel(sum_ref, kernel_ref, norm_ref):
    total = sum(sum_ref[p] for p in range(sum_ref.shape[0]))
    block = total.shape[0]
    average = total / total[:, 3 * K + 6 : 3 * K + 7]
    average = jnp.concatenate([average, jnp.zeros((LANES - block, LANES), jnp.float32)], axis=0)
    turned = average.T
    for b in range(3):
        kernel_ref[:, b * block : (b + 1) * block] = turned[b * K : (b + 1) * K, :block]
        norm_ref[:, b * block : (b + 1) * block] = turned[3 * K + 2 * b : 3 * K + 2 * b + 2, :block]


def on_device(glu_in, cotangent, frame_count, kernel, norm_params, drift_kernel, drift_norm):
    channels = cotangent.shape[1]
    tiles = channels // LANES
    n_dp = lax.axis_size("dp")
    n_group = lax.axis_size("group")
    peers = n_dp // 2
    share = channels // n_dp
    same_core = [[2 * p + core for p in range(peers)] for core in range(2)]
    swap = [(i, i ^ 1) for i in range(n_dp)]
    vmem = pl.BlockSpec(memory_space=pltpu.VMEM)
    smem = pl.BlockSpec(memory_space=pltpu.SMEM)
    params = pltpu.CompilerParams(vmem_limit_bytes=48 * 1024 * 1024)
    f32 = jnp.float32

    padded, conv_out, stats = pl.pallas_call(
        conv_kernel,
        out_shape=(
            jax.ShapeDtypeStruct((UTT * PADDED, channels), f32),
            jax.ShapeDtypeStruct((ROWS, channels), f32),
            jax.ShapeDtypeStruct((STAT_ROWS, LANES), f32),
        ),
        in_specs=[smem, vmem, vmem],
        out_specs=(vmem, vmem, vmem),
        scratch_shapes=[pltpu.VMEM((K, channels), f32)],
        compiler_params=params,
        name="conv_stats",
    )(frame_count, glu_in, kernel)

    other = lax.ppermute(stats, "dp", swap)
    spread_out = pl.pallas_call(
        functools.partial(pair_kernel, tiles),
        out_shape=jax.ShapeDtypeStruct((peers, STAT_ROWS, LANES), f32),
        in_specs=[vmem, vmem],
        out_specs=vmem,
        compiler_params=params,
        name="pair_stats",
    )(stats, other)
    gathered = lax.all_to_all(spread_out, "dp", 0, 0, axis_index_groups=same_core)

    both = pl.pallas_call(
        back_kernel,
        out_shape=jax.ShapeDtypeStruct((2, peers, share, LANES), f32),
        in_specs=[smem, vmem, vmem, vmem, vmem, vmem],
        out_specs=vmem,
        scratch_shapes=[
            pltpu.VMEM((16, LANES), f32),
            pltpu.VMEM((16, LANES), f32),
            pltpu.VMEM((2, channels), f32),
            pltpu.VMEM((channels, LANES), f32),
        ],
        compiler_params=params,
        name="tap_sums",
    )(frame_count, gathered, cotangent, norm_params, padded, conv_out)
    arrived = lax.ppermute(both[1], "dp", swap)
    tap_sums = lax.all_to_all(both[0] + arrived, "dp", 0, 0, axis_index_groups=same_core)

    weighted = pl.pallas_call(
        delta_kernel,
        out_shape=jax.ShapeDtypeStruct((n_group, share // 3, LANES), f32),
        in_specs=[vmem, vmem, vmem],
        out_specs=vmem,
        compiler_params=params,
        name="group_delta",
    )(tap_sums, drift_kernel, drift_norm)
    weighted = lax.all_to_all(weighted, "group", 0, 0)

    return pl.pallas_call(
        average_kernel,
        out_shape=(
            jax.ShapeDtypeStruct((K, share), f32),
            jax.ShapeDtypeStruct((2, share), f32),
        ),
        in_specs=[vmem],
        out_specs=(vmem, vmem),
        compiler_params=params,
        name="group_average",
    )(weighted)


def solution(mesh):
    placed = (
        P(("dp", "group"), None),
        P(("dp", "group"), None),
        P(("dp", "group")),
        P("group", None, None),
        P("group", None, None),
        P("group", None, None),
        P("group", None, None),
    )
    return jax.shard_map(
        on_device,
        mesh=mesh,
        in_specs=placed,
        out_specs=(P(None, "dp"), P(None, "dp")),
        check_vma=False,
    )
```

```python
import functools
import operator

import jax
import jax.numpy as jnp
from jax import lax
from jax.experimental import pallas as pl
from jax.experimental.pallas import tpu as pltpu
from jax.sharding import PartitionSpec as P

K = 32
HALF = K // 2
SUB = 8
LANES = 128
SLOT = 128
UTT = 2
ROWS = UTT * SLOT
PADDED = HALF + SLOT + HALF
STAT_ROWS = 32
CHUNKS = (4, 8)
R_STEP = 8
UNROLL = 4
TILE_RUN = 3

grad_factor_base = 128.0
eps_norm = 1e-05


def lane_tile(i):
    return pl.ds(pl.multiple_of(i * LANES, LANES), LANES)


def live_rows(count):
    return lax.broadcasted_iota(jnp.int32, (SLOT, LANES), 0) < count


def added(terms):
    return functools.reduce(operator.add, terms)


def fold_rows(field):
    return jnp.sum(field.reshape(field.shape[0] // SUB, SUB, LANES), axis=0)


def scan_rows(field, upward):
    row = lax.broadcasted_iota(jnp.int32, field.shape, 0)
    step = 1
    while step < HALF:
        if upward:
            moved = jnp.where(row < HALF - step, pltpu.roll(field, HALF - step, 0), 0.0)
        else:
            moved = jnp.where(row >= step, pltpu.roll(field, step, 0), 0.0)
        field = field + moved
        step *= 2
    return field


PLAIN, NEXT, SECOND, BOTH = range(4)
PRODUCTS = (
    (PLAIN, 3),
    (SECOND, 1),
    (SECOND, 3),
    (NEXT, 2),
    (BOTH, 0),
    (BOTH, 2),
    (NEXT, 3),
    (BOTH, 1),
    (BOTH, 3),
)
COMBOS = ((0, 1, 2, 3), (0, 1), (2, 3), (0, 2), (0,), (2,), (1, 3), (1,), (3,))


def combine(parts):
    low = parts[0] + parts[1]
    high = parts[0] - parts[2]
    return (
        low + (parts[3] + parts[4]),
        low - (parts[6] + parts[7]),
        high + (parts[3] - parts[5]),
        high - (parts[6] - parts[8]),
    )


def fields_at(field_ref, i, row, product):
    kind, block = product
    return [
        field_ref[i, kind, pl.ds(row + SUB * (4 * m + block), SUB), :] for m in range(SLOT // SUB // 4)
    ]


def conv_kernel(
    count_hbm,
    glu_hbm,
    kernel_hbm,
    cot_hbm,
    field_ref,
    conv_ref,
    stat_ref,
    cot_ref,
    live_sum_ref,
    live_ref,
    count_ref,
    glu_ref,
    kernel_ref,
    taps_ref,
    small_sems,
    glu_sems,
):
    tiles = conv_ref.shape[0]
    channels = tiles * LANES
    count_copy = pltpu.make_async_copy(count_hbm, count_ref, small_sems.at[0])
    kernel_copy = pltpu.make_async_copy(kernel_hbm, kernel_ref, small_sems.at[1])
    cot_copy = pltpu.make_async_copy(cot_hbm, cot_ref, small_sems.at[2])
    glu_copies = []
    for c, count in enumerate(CHUNKS):
        for half in range(2):
            columns = pl.ds(half * channels + sum(CHUNKS[:c]) * LANES, count * LANES)
            glu_copies.append(
                pltpu.make_async_copy(
                    glu_hbm.at[:, columns], glu_ref.at[:, columns], glu_sems.at[c, half]
                )
            )
    count_copy.start()
    kernel_copy.start()
    for copy in glu_copies:
        copy.start()
    cot_copy.start()
    count_copy.wait()
    counts = [count_ref[u] for u in range(UTT)]
    local_frames = sum(counts).astype(jnp.float32)
    stat_ref[...] = jnp.full(stat_ref.shape, local_frames, jnp.float32)
    for u in range(UTT):
        live_ref[pl.ds(u * SLOT, SLOT), :] = jnp.where(live_rows(counts[u]), 1.0, 0.0)
    kernel_copy.wait()
    for i in range(tiles):
        rows = kernel_ref[0, :, i * LANES : (i + 1) * LANES].astype(jnp.float32)
        rows = [rows[SUB * j : SUB * (j + 1)] for j in range(K // SUB)]
        for n, combo in enumerate(COMBOS):
            taps_ref[i, n] = added([rows[j] for j in combo])

    def tile(i, carry):
        lanes = lane_tile(i)
        gate_lanes = lane_tile(i + tiles)
        edge = jnp.zeros((HALF, LANES), jnp.float32)
        field_sum = jnp.zeros((SUB, LANES), jnp.float32)
        head = edge
        tail = edge
        total = jnp.zeros((SUB, LANES), jnp.float32)
        for u in range(UTT):
            rows = pl.ds(u * SLOT, SLOT)
            base = u * PADDED
            value = glu_ref[rows, lanes].astype(jnp.float32)
            gate = glu_ref[rows, gate_lanes].astype(jnp.float32)
            field = value * jax.nn.sigmoid(gate) * live_ref[rows, :]
            field_sum = field_sum + fold_rows(field)
            head = head + field[:HALF]
            field = jnp.concatenate([edge, field, edge], axis=0)
            near = field[: PADDED - SUB] - field[SUB:]
            field_ref[i, PLAIN, pl.ds(base, PADDED), :] = field
            field_ref[i, NEXT, pl.ds(base, PADDED - SUB), :] = near
            field_ref[i, SECOND, pl.ds(base, PADDED - 2 * SUB), :] = (
                field[: PADDED - 2 * SUB] - field[2 * SUB :]
            )
            field_ref[i, BOTH, pl.ds(base, PADDED - 3 * SUB), :] = (
                near[: PADDED - 3 * SUB] - near[2 * SUB :]
            )
            tail = tail + field_ref[i, PLAIN, pl.ds(base + counts[u], HALF), :]

        for u in range(UTT):
            base = u * PADDED

            def taps(step, sums):
                sums = list(sums)
                for r in range(R_STEP):
                    first = step * R_STEP + r
                    for n, product in enumerate(PRODUCTS):
                        tap = taps_ref[i, n, pl.ds(first, 1), :]
                        for m, field in enumerate(fields_at(field_ref, i, base + first, product)):
                            sums[4 * n + m] = sums[4 * n + m] + field * tap
                return tuple(sums)

            zero = jnp.zeros((SUB, LANES), jnp.float32)
            sums = lax.fori_loop(0, SUB // R_STEP, taps, (zero,) * (4 * len(PRODUCTS)))
            for m in range(SLOT // SUB // 4):
                for q, out in enumerate(combine(sums[m::4])):
                    at = pl.ds(u * SLOT + SUB * (4 * m + q), SUB)
                    conv_ref[i, at, :] = out
                    total = total + out * live_ref[at, :]
        local_mean = jnp.sum(total, axis=0, keepdims=True) / local_frames
        spread = jnp.zeros((SUB, LANES), jnp.float32)
        for u in range(UTT):
            rows = pl.ds(u * SLOT, SLOT)
            centered = (conv_ref[i, rows, :] - local_mean) * live_ref[rows, :]
            spread = spread + fold_rows(centered * centered)
        stat_ref[pl.ds(i, 1), :] = local_mean
        stat_ref[pl.ds(i + tiles, 1), :] = jnp.sum(spread, axis=0, keepdims=True)
        live_sum_ref[i] = jnp.sum(field_sum, axis=0, keepdims=True) - jnp.concatenate(
            [scan_rows(tail, True), scan_rows(head, False) - head], axis=0
        )
        return carry

    for c, count in enumerate(CHUNKS):
        glu_copies[2 * c].wait()
        glu_copies[2 * c + 1].wait()
        lax.fori_loop(sum(CHUNKS[:c]), sum(CHUNKS[: c + 1]), tile, 0, unroll=UNROLL)
    cot_copy.wait()


def merge_stats(parts, tiles):
    frames = added([part[2 * tiles : 2 * tiles + 1] for part in parts])
    mean = added([part[:tiles] * part[2 * tiles : 2 * tiles + 1] for part in parts]) / frames
    spread = added(
        [
            part[tiles : 2 * tiles]
            + part[2 * tiles : 2 * tiles + 1] * (part[:tiles] - mean) * (part[:tiles] - mean)
            for part in parts
        ]
    )
    return frames, mean, spread


def pair_kernel(tiles, own_ref, other_ref, out_ref):
    frames, mean, spread = merge_stats([own_ref[...], other_ref[...]], tiles)
    rest = jnp.broadcast_to(frames, (STAT_ROWS - 2 * tiles, LANES))
    for peer in range(out_ref.shape[0]):
        out_ref[peer, pl.ds(0, tiles), :] = mean
        out_ref[peer, pl.ds(tiles, tiles), :] = spread
        out_ref[peer, pl.ds(2 * tiles, STAT_ROWS - 2 * tiles), :] = rest


def back_kernel(
    stat_ref,
    own_ref,
    cot_ref,
    param_ref,
    field_ref,
    conv_ref,
    live_sum_ref,
    live_ref,
    out_ref,
    mean_ref,
    inv_ref,
    par_ref,
    tap_ref,
):
    tiles = conv_ref.shape[0]
    channels = tiles * LANES
    frames, mean, spread = merge_stats([stat_ref[p] for p in range(stat_ref.shape[0])], tiles)
    mean_ref[pl.ds(0, tiles), :] = mean
    inv_ref[pl.ds(0, tiles), :] = lax.rsqrt(spread / frames + eps_norm)
    par_ref[...] = param_ref[0].astype(jnp.float32)
    local_frames = own_ref[pl.ds(2 * tiles, 1), :]

    def tile(i):
        lanes = lane_tile(i)
        mean_row = mean_ref[pl.ds(i, 1), :]
        inv_row = inv_ref[pl.ds(i, 1), :]
        gain_row = par_ref[pl.ds(0, 1), lanes]
        shift_row = par_ref[pl.ds(1, 1), lanes]
        gain_sum = jnp.zeros((SUB, LANES), jnp.float32)
        shift_sum = jnp.zeros((SUB, LANES), jnp.float32)
        for u in range(UTT):
            rows = pl.ds(u * SLOT, SLOT)
            base = u * PADDED
            live = live_ref[rows, :]
            normed = (conv_ref[i, rows, :] - mean_row) * inv_row
            norm_out = gain_row * normed + shift_row
            sig = jax.nn.sigmoid(norm_out)
            slope = sig * (1.0 + norm_out * (1.0 - sig))
            upstream = cot_ref[rows, lanes].astype(jnp.float32) * slope * live
            normed = normed * live
            gain_sum = gain_sum + fold_rows(upstream * normed)
            shift_sum = shift_sum + fold_rows(upstream)
            for which, source in enumerate((upstream, normed)):
                blocks = [source[SUB * q : SUB * (q + 1)] for q in range(SLOT // SUB)]
                mixes = [
                    [added([blocks[4 * m + q] for q in combo]) for m in range(SLOT // SUB // 4)]
                    for combo in COMBOS
                ]

                def taps(step, carry):
                    for r in range(R_STEP):
                        first = step * R_STEP + r
                        parts = []
                        for mix, product in zip(mixes, PRODUCTS):
                            fields = fields_at(field_ref, i, base + first, product)
                            parts.append(added([x * field for x, field in zip(mix, fields)]))
                        for j, out in enumerate(combine(parts)):
                            at = pl.ds(SUB * (which * K + first + SUB * j), SUB)
                            tap_ref[at, :] = out if u == 0 else tap_ref[at, :] + out
                    return carry

                lax.fori_loop(0, SUB // R_STEP, taps, 0)
        scale = gain_row * inv_row
        tap_rows = added([tap_ref[pl.ds(row, 2 * K, stride=SUB), :] for row in range(SUB)])
        row = lax.broadcasted_iota(jnp.int32, (K, LANES), 0)
        extra = jnp.where(row == 0, jnp.sum(gain_sum, axis=0, keepdims=True), local_frames)
        extra = jnp.where(row == 1, jnp.sum(shift_sum, axis=0, keepdims=True), extra)
        block = jnp.concatenate(
            [tap_rows[:K] * scale, live_sum_ref[i] * scale, tap_rows[K:] * scale, extra], axis=0
        )
        return block.T

    core = lax.rem(lax.axis_index("dp"), 2)
    share = channels // (2 * out_ref.shape[1])
    pairs = TILE_RUN * LANES // share // 2

    def run(step, carry):
        turned = jnp.concatenate([tile(step * TILE_RUN + n) for n in range(TILE_RUN)], axis=0)
        for j in range(2 * pairs):
            side = core if j % 2 == 0 else 1 - core
            out_ref[side, step * pairs + j // 2] = turned[j * share : (j + 1) * share]
        return carry

    lax.fori_loop(0, tiles // TILE_RUN, run, 0)


def delta_kernel(sum_ref, drift_ref, drift_norm_ref, out_ref):
    share = sum_ref.shape[1]
    channels = drift_ref.shape[2]
    total = added([sum_ref[p] for p in range(sum_ref.shape[0])])
    frames = total[:, 3 * K + 2 : 3 * K + 3]
    gain_sum = total[:, 3 * K : 3 * K + 1]
    shift_sum = total[:, 3 * K + 1 : 3 * K + 2]
    live_part = pltpu.roll(total, LANES - K, 1)
    norm_part = pltpu.roll(total, LANES - 2 * K, 1)
    kernel_sum = total - (shift_sum * live_part + gain_sum * norm_part) / frames
    start = lax.axis_index("dp") * share
    first = jnp.minimum(start // LANES, channels // LANES - 2)
    window = pl.ds(pl.multiple_of(first * LANES, LANES), 2 * LANES)
    drift = jnp.concatenate(
        [
            drift_ref[0, :, window].astype(jnp.float32),
            drift_norm_ref[0, :, window].astype(jnp.float32),
            jnp.zeros((LANES - K - 2, 2 * LANES), jnp.float32),
        ],
        axis=0,
    )
    drift = pltpu.roll(drift, lax.rem(2 * LANES - (start - first * LANES), 2 * LANES), 1)
    drift = drift[:, :LANES].T[:share]
    lane = lax.broadcasted_iota(jnp.int32, (share, LANES), 1)
    norm_at = pltpu.roll(total, LANES - 2 * K, 1)
    sums = jnp.where(lane < K, kernel_sum, norm_at)
    delta = (drift + (grad_factor_base / frames) * sums).astype(jnp.bfloat16).astype(jnp.float32)
    weighted = delta * frames
    block = share // 3
    lane = lane[:block]
    packed = jnp.broadcast_to(frames[:block], (block, LANES))
    for b in range(3):
        piece = weighted[b * block : (b + 1) * block]
        moved = pltpu.roll(piece, b * K, 1) if b else piece
        packed = jnp.where((lane >= b * K) & (lane < (b + 1) * K), moved, packed)
        at = 3 * K + 2 * b
        moved = pltpu.roll(piece, at - K, 1)
        packed = jnp.where((lane >= at) & (lane < at + 2), moved, packed)
    for peer in range(out_ref.shape[0]):
        out_ref[peer] = packed


def average_kernel(sum_ref, kernel_ref, norm_ref):
    total = added([sum_ref[p] for p in range(sum_ref.shape[0])])
    block = total.shape[0]
    average = total / total[:, 3 * K + 6 : 3 * K + 7]
    average = jnp.concatenate([average, jnp.zeros((LANES - block, LANES), jnp.float32)], axis=0)
    turned = average.T
    for b in range(3):
        kernel_ref[:, b * block : (b + 1) * block] = turned[b * K : (b + 1) * K, :block]
        norm_ref[:, b * block : (b + 1) * block] = turned[3 * K + 2 * b : 3 * K + 2 * b + 2, :block]


VMEM_SPEC = pl.BlockSpec(memory_space=pltpu.VMEM)
HBM_SPEC = pl.BlockSpec(memory_space=pltpu.HBM)
PARAMS = pltpu.CompilerParams(vmem_limit_bytes=32 * 1024 * 1024)


def conv_stage(frame_count, glu_in, kernel, cotangent):
    tiles = cotangent.shape[1] // LANES
    far = [
        pltpu.with_memory_space_constraint(x, pltpu.HBM)
        for x in (frame_count, glu_in, kernel, cotangent)
    ]
    return pl.pallas_call(
        conv_kernel,
        out_shape=(
            jax.ShapeDtypeStruct((tiles, 4, UTT * PADDED, LANES), jnp.float32),
            jax.ShapeDtypeStruct((tiles, ROWS, LANES), jnp.float32),
            jax.ShapeDtypeStruct((STAT_ROWS, LANES), jnp.float32),
            jax.ShapeDtypeStruct(cotangent.shape, cotangent.dtype),
            jax.ShapeDtypeStruct((tiles, K, LANES), jnp.float32),
            jax.ShapeDtypeStruct((ROWS, LANES), jnp.float32),
        ),
        in_specs=[HBM_SPEC] * 4,
        out_specs=(VMEM_SPEC,) * 6,
        scratch_shapes=[
            pltpu.SMEM((UTT,), jnp.int32),
            pltpu.VMEM(glu_in.shape, glu_in.dtype),
            pltpu.VMEM(kernel.shape, kernel.dtype),
            pltpu.VMEM((tiles, len(PRODUCTS), SUB, LANES), jnp.float32),
            pltpu.SemaphoreType.DMA((3,)),
            pltpu.SemaphoreType.DMA((len(CHUNKS), 2)),
        ],
        compiler_params=PARAMS,
        name="conv_stats",
    )(*far)


def pair_stage(stats, other, peers, tiles):
    return pl.pallas_call(
        functools.partial(pair_kernel, tiles),
        out_shape=jax.ShapeDtypeStruct((peers, STAT_ROWS, LANES), jnp.float32),
        in_specs=[VMEM_SPEC] * 2,
        out_specs=VMEM_SPEC,
        compiler_params=PARAMS,
        name="pair_stats",
    )(stats, other)


def back_stage(gathered, stats, cotangent, norm_params, fields, conv_out, live_sum, live):
    channels = cotangent.shape[1]
    peers = gathered.shape[0]
    return pl.pallas_call(
        back_kernel,
        out_shape=jax.ShapeDtypeStruct((2, peers, channels // (2 * peers), LANES), jnp.float32),
        in_specs=[VMEM_SPEC] * 8,
        out_specs=VMEM_SPEC,
        scratch_shapes=[
            pltpu.VMEM((16, LANES), jnp.float32),
            pltpu.VMEM((16, LANES), jnp.float32),
            pltpu.VMEM((2, channels), jnp.float32),
            pltpu.VMEM((2 * K * SUB, LANES), jnp.float32),
        ],
        compiler_params=PARAMS,
        name="tap_sums",
    )(gathered, stats, cotangent, norm_params, fields, conv_out, live_sum, live)


def on_device(glu_in, cotangent, frame_count, kernel, norm_params, drift_kernel, drift_norm):
    channels = cotangent.shape[1]
    tiles = channels // LANES
    n_dp = lax.axis_size("dp")
    n_group = lax.axis_size("group")
    peers = n_dp // 2
    share = channels // n_dp
    same_core = [[2 * p + core for p in range(peers)] for core in range(2)]
    swap = [(i, i ^ 1) for i in range(n_dp)]

    fields, conv_out, stats, cot_near, live_sum, live = conv_stage(
        frame_count, glu_in, kernel, cotangent
    )
    other = lax.ppermute(stats, "dp", swap)
    spread_out = pair_stage(stats, other, peers, tiles)
    gathered = lax.all_to_all(spread_out, "dp", 0, 0, axis_index_groups=same_core)

    both = back_stage(gathered, stats, cot_near, norm_params, fields, conv_out, live_sum, live)
    arrived = lax.ppermute(both[1], "dp", swap)
    tap_sums = lax.all_to_all(both[0] + arrived, "dp", 0, 0, axis_index_groups=same_core)

    weighted = pl.pallas_call(
        delta_kernel,
        out_shape=jax.ShapeDtypeStruct((n_group, share // 3, LANES), jnp.float32),
        in_specs=[VMEM_SPEC] * 3,
        out_specs=VMEM_SPEC,
        compiler_params=PARAMS,
        name="group_delta",
    )(tap_sums, drift_kernel, drift_norm)
    weighted = lax.all_to_all(weighted, "group", 0, 0)

    return pl.pallas_call(
        average_kernel,
        out_shape=(
            jax.ShapeDtypeStruct((K, share), jnp.float32),
            jax.ShapeDtypeStruct((2, share), jnp.float32),
        ),
        in_specs=[VMEM_SPEC],
        out_specs=(VMEM_SPEC, VMEM_SPEC),
        compiler_params=PARAMS,
        name="group_average",
    )(weighted)


def solution(mesh):
    placed = (
        P(("dp", "group"), None),
        P(("dp", "group"), None),
        P(("dp", "group")),
        P("group", None, None),
        P("group", None, None),
        P("group", None, None),
        P("group", None, None),
    )
    return jax.shard_map(
        on_device,
        mesh=mesh,
        in_specs=placed,
        out_specs=(P(None, "dp"), P(None, "dp")),
        check_vma=False,
    )
```

```python
import functools
import operator

import jax
import jax.numpy as jnp
from jax import lax
from jax.experimental import pallas as pl
from jax.experimental.pallas import tpu as pltpu
from jax.sharding import PartitionSpec as P

K = 32
HALF = K // 2
SUB = 8
LANES = 128
SLOT = 128
UTT = 2
ROWS = UTT * SLOT
PADDED = HALF + SLOT + HALF
CHUNKS = (4, 8)
R_STEP = 8
UNROLL = 4
TILE_RUN = 3

grad_factor_base = 128.0
eps_norm = 1e-05


def lane_tile(i):
    return pl.ds(pl.multiple_of(i * LANES, LANES), LANES)


def peer_rows(row, peers, tiles):
    return pl.ds(row, peers, stride=2 * tiles + 1)


def live_rows(count):
    return lax.broadcasted_iota(jnp.int32, (SLOT, LANES), 0) < count


def added(terms):
    return functools.reduce(operator.add, terms)


def fold_rows(field):
    return jnp.sum(field.reshape(field.shape[0] // SUB, SUB, LANES), axis=0)


def scan_rows(field, upward):
    row = lax.broadcasted_iota(jnp.int32, field.shape, 0)
    step = 1
    while step < HALF:
        if upward:
            moved = jnp.where(row < HALF - step, pltpu.roll(field, HALF - step, 0), 0.0)
        else:
            moved = jnp.where(row >= step, pltpu.roll(field, step, 0), 0.0)
        field = field + moved
        step *= 2
    return field


PLAIN, NEXT, SECOND, BOTH = range(4)
PRODUCTS = (
    (PLAIN, 3),
    (SECOND, 1),
    (SECOND, 3),
    (NEXT, 2),
    (BOTH, 0),
    (BOTH, 2),
    (NEXT, 3),
    (BOTH, 1),
    (BOTH, 3),
)
COMBOS = ((0, 1, 2, 3), (0, 1), (2, 3), (0, 2), (0,), (2,), (1, 3), (1,), (3,))


def combine(parts):
    low = parts[0] + parts[1]
    high = parts[0] - parts[2]
    return (
        low + (parts[3] + parts[4]),
        low - (parts[6] + parts[7]),
        high + (parts[3] - parts[5]),
        high - (parts[6] - parts[8]),
    )


def fields_at(field_ref, i, row, product):
    kind, block = product
    return [
        field_ref[i, kind, pl.ds(row + SUB * (4 * m + block), SUB), :] for m in range(SLOT // SUB // 4)
    ]


def conv_kernel(
    count_hbm,
    glu_hbm,
    kernel_hbm,
    cot_hbm,
    field_ref,
    conv_ref,
    stat_ref,
    cot_ref,
    live_sum_ref,
    live_ref,
    count_ref,
    glu_ref,
    kernel_ref,
    taps_ref,
    small_sems,
    glu_sems,
):
    tiles = conv_ref.shape[0]
    channels = tiles * LANES
    count_copy = pltpu.make_async_copy(count_hbm, count_ref, small_sems.at[0])
    kernel_copy = pltpu.make_async_copy(kernel_hbm, kernel_ref, small_sems.at[1])
    cot_copy = pltpu.make_async_copy(cot_hbm, cot_ref, small_sems.at[2])
    glu_copies = []
    for c, count in enumerate(CHUNKS):
        for half in range(2):
            columns = pl.ds(half * channels + sum(CHUNKS[:c]) * LANES, count * LANES)
            glu_copies.append(
                pltpu.make_async_copy(
                    glu_hbm.at[:, columns], glu_ref.at[:, columns], glu_sems.at[c, half]
                )
            )
    count_copy.start()
    kernel_copy.start()
    for copy in glu_copies:
        copy.start()
    cot_copy.start()
    count_copy.wait()
    counts = [count_ref[u] for u in range(UTT)]
    local_frames = sum(counts).astype(jnp.float32)
    stat_ref[...] = jnp.full(stat_ref.shape, local_frames, jnp.float32)
    for u in range(UTT):
        live_ref[pl.ds(u * SLOT, SLOT), :] = jnp.where(live_rows(counts[u]), 1.0, 0.0)
    kernel_copy.wait()
    for i in range(tiles):
        rows = kernel_ref[0, :, i * LANES : (i + 1) * LANES].astype(jnp.float32)
        rows = [rows[SUB * j : SUB * (j + 1)] for j in range(K // SUB)]
        for n, combo in enumerate(COMBOS):
            taps_ref[i, n] = added([rows[j] for j in combo])

    def tile(i, carry):
        lanes = lane_tile(i)
        gate_lanes = lane_tile(i + tiles)
        edge = jnp.zeros((HALF, LANES), jnp.float32)
        field_sum = jnp.zeros((SUB, LANES), jnp.float32)
        head = edge
        tail = edge
        total = jnp.zeros((SUB, LANES), jnp.float32)
        for u in range(UTT):
            rows = pl.ds(u * SLOT, SLOT)
            base = u * PADDED
            value = glu_ref[rows, lanes].astype(jnp.float32)
            gate = glu_ref[rows, gate_lanes].astype(jnp.float32)
            field = value * jax.nn.sigmoid(gate) * live_ref[rows, :]
            field_sum = field_sum + fold_rows(field)
            head = head + field[:HALF]
            field = jnp.concatenate([edge, field, edge], axis=0)
            near = field[: PADDED - SUB] - field[SUB:]
            field_ref[i, PLAIN, pl.ds(base, PADDED), :] = field
            field_ref[i, NEXT, pl.ds(base, PADDED - SUB), :] = near
            field_ref[i, SECOND, pl.ds(base, PADDED - 2 * SUB), :] = (
                field[: PADDED - 2 * SUB] - field[2 * SUB :]
            )
            field_ref[i, BOTH, pl.ds(base, PADDED - 3 * SUB), :] = (
                near[: PADDED - 3 * SUB] - near[2 * SUB :]
            )
            tail = tail + field_ref[i, PLAIN, pl.ds(base + counts[u], HALF), :]

        for u in range(UTT):
            base = u * PADDED

            def taps(step, sums):
                sums = list(sums)
                for r in range(R_STEP):
                    first = step * R_STEP + r
                    for n, product in enumerate(PRODUCTS):
                        tap = taps_ref[i, n, pl.ds(first, 1), :]
                        for m, field in enumerate(fields_at(field_ref, i, base + first, product)):
                            sums[4 * n + m] = sums[4 * n + m] + field * tap
                return tuple(sums)

            zero = jnp.zeros((SUB, LANES), jnp.float32)
            sums = lax.fori_loop(0, SUB // R_STEP, taps, (zero,) * (4 * len(PRODUCTS)))
            for m in range(SLOT // SUB // 4):
                for q, out in enumerate(combine(sums[m::4])):
                    at = pl.ds(u * SLOT + SUB * (4 * m + q), SUB)
                    conv_ref[i, at, :] = out
                    total = total + out * live_ref[at, :]
        local_mean = jnp.sum(total, axis=0, keepdims=True) / local_frames
        spread = jnp.zeros((SUB, LANES), jnp.float32)
        for u in range(UTT):
            rows = pl.ds(u * SLOT, SLOT)
            centered = (conv_ref[i, rows, :] - local_mean) * live_ref[rows, :]
            spread = spread + fold_rows(centered * centered)
        stat_ref[pl.ds(i, 1), :] = local_mean
        stat_ref[pl.ds(i + tiles, 1), :] = jnp.sum(spread, axis=0, keepdims=True)
        live_sum_ref[i] = jnp.sum(field_sum, axis=0, keepdims=True) - jnp.concatenate(
            [scan_rows(tail, True), scan_rows(head, False) - head], axis=0
        )
        return carry

    for c, count in enumerate(CHUNKS):
        glu_copies[2 * c].wait()
        glu_copies[2 * c + 1].wait()
        lax.fori_loop(sum(CHUNKS[:c]), sum(CHUNKS[: c + 1]), tile, 0, unroll=UNROLL)
    cot_copy.wait()


def pair_kernel(own_ref, other_ref, out_ref):
    rows = own_ref.shape[0] - SUB + 1
    tiles = rows // 2
    parts = [ref[...] for ref in (own_ref, other_ref)]
    counts = [part[2 * tiles : 2 * tiles + 1] for part in parts]
    frames = counts[0] + counts[1]
    means = [part[:tiles] for part in parts]
    mean = (counts[0] * means[0] + counts[1] * means[1]) / frames
    spread = added(
        [part[tiles : 2 * tiles] + n * (m - mean) * (m - mean) for part, n, m in zip(parts, counts, means)]
    )
    merged = jnp.concatenate([mean, spread, jnp.broadcast_to(frames, (SUB, LANES))], axis=0)
    for peer in range(out_ref.shape[0] // rows):
        out_ref[pl.ds(peer * rows, rows), :] = merged[:rows]


def store_taps(tap_ref, field_ref, i, u, source):
    blocks = [source[SUB * q : SUB * (q + 1)] for q in range(SLOT // SUB)]
    mixes = [
        [added([blocks[4 * m + q] for q in combo]) for m in range(SLOT // SUB // 4)]
        for combo in COMBOS
    ]
    for first in range(SUB):
        parts = []
        for mix, product in zip(mixes, PRODUCTS):
            fields = fields_at(field_ref, i, u * PADDED + first, product)
            parts.append(added([x * field for x, field in zip(mix, fields)]))
        for j, out in enumerate(combine(parts)):
            at = pl.ds(SUB * (first + SUB * j), SUB)
            tap_ref[at, :] = out if u == 0 else tap_ref[at, :] + out


def load_taps(tap_ref):
    return added([tap_ref[pl.ds(row, K, stride=SUB), :] for row in range(SUB)])


def lane_in(low, high):
    lane = lax.broadcasted_iota(jnp.int32, (SUB, LANES), 1)
    return (lane >= low) & (lane < high)


def pack_chunk(chunk):
    blocks = [chunk[SUB * b : SUB * (b + 1)] for b in range(6)]
    last = pltpu.roll(blocks[5], 3 * K, 1)
    moved = [pltpu.roll(blocks[4], (3 - n) * K, 1) for n in range(3)] + [last]
    packed = [jnp.where(lane_in(0, 3 * K), blocks[n], moved[n]) for n in range(4)]
    for b in range(6):
        extra = pltpu.roll(blocks[b], LANES - K + 2 * b, 1)
        last = jnp.where(lane_in(2 * K + 2 * b, 2 * K + 2 * b + 3), extra, last)
    return packed + [last]


def unpack_chunk(packed):
    parts = [packed[SUB * n : SUB * (n + 1)] for n in range(5)]
    four = pltpu.roll(parts[0], K, 1)
    four = jnp.where(lane_in(K, 2 * K), pltpu.roll(parts[1], 2 * K, 1), four)
    four = jnp.where(lane_in(2 * K, 3 * K), pltpu.roll(parts[2], 3 * K, 1), four)
    five = jnp.where(lane_in(0, K), pltpu.roll(parts[3], K, 1), pltpu.roll(parts[4], K, 1))
    sums = jnp.concatenate(parts[:4] + [four, five], axis=0)
    at = [2 * K + 2 * b for b in range(6)]
    gain_sum = jnp.concatenate([parts[4][:, n : n + 1] for n in at], axis=0)
    shift_sum = jnp.concatenate([parts[4][:, n + 1 : n + 2] for n in at], axis=0)
    return sums, gain_sum, shift_sum, parts[4][:1, at[5] + 2 : at[5] + 3]


def back_kernel(
    stat_ref,
    own_ref,
    cot_ref,
    param_ref,
    field_ref,
    conv_ref,
    live_sum_ref,
    live_ref,
    out_ref,
    par_ref,
    up_ref,
    norm_ref,
):
    tiles = conv_ref.shape[0]
    pairs = out_ref.shape[1]
    share = tiles * LANES // (2 * pairs)
    per_run = TILE_RUN * LANES // share
    core = lax.rem(lax.axis_index("dp"), 2)
    par_ref[...] = param_ref[0].astype(jnp.float32)
    local_frames = own_ref[pl.ds(2 * tiles, 1), :]
    counts = stat_ref[peer_rows(2 * tiles, pairs, tiles), :]
    frames = jnp.sum(counts, axis=0, keepdims=True)
    row = lax.broadcasted_iota(jnp.int32, (SUB, LANES), 0)
    rest = jnp.zeros((K - SUB, LANES), jnp.float32)

    def tile(i):
        lanes = lane_tile(i)
        means = stat_ref[peer_rows(i, pairs, tiles), :]
        mean_row = jnp.sum(counts * means, axis=0, keepdims=True) / frames
        apart = means - mean_row
        spread = stat_ref[peer_rows(i + tiles, pairs, tiles), :] + counts * apart * apart
        inv_row = lax.rsqrt(jnp.sum(spread, axis=0, keepdims=True) / frames + eps_norm)
        gain_row = par_ref[pl.ds(0, 1), lanes]
        shift_row = par_ref[pl.ds(1, 1), lanes]
        gain_sum = jnp.zeros((SUB, LANES), jnp.float32)
        shift_sum = jnp.zeros((SUB, LANES), jnp.float32)
        for u in range(UTT):
            rows = pl.ds(u * SLOT, SLOT)
            live = live_ref[rows, :]
            normed = (conv_ref[i, rows, :] - mean_row) * inv_row
            norm_out = gain_row * normed + shift_row
            sig = jax.nn.sigmoid(norm_out)
            slope = sig * (1.0 + norm_out * (1.0 - sig))
            upstream = cot_ref[rows, lanes].astype(jnp.float32) * slope * live
            normed = normed * live
            gain_sum = gain_sum + fold_rows(upstream * normed)
            shift_sum = shift_sum + fold_rows(upstream)
            store_taps(up_ref, field_ref, i, u, upstream)
            store_taps(norm_ref, field_ref, i, u, normed)
        scale = gain_row * inv_row
        extra = jnp.where(row == 0, jnp.sum(gain_sum, axis=0, keepdims=True), local_frames)
        extra = jnp.where(row == 1, jnp.sum(shift_sum, axis=0, keepdims=True), extra)
        block = jnp.concatenate(
            [
                load_taps(up_ref) * scale,
                live_sum_ref[i] * scale,
                load_taps(norm_ref) * scale,
                extra,
                rest,
            ],
            axis=0,
        )
        return block.T

    def run(step, carry):
        turned = jnp.concatenate([tile(step * TILE_RUN + n) for n in range(TILE_RUN)], axis=0)
        for j in range(per_run):
            side = core if j % 2 == 0 else 1 - core
            chunk = turned[j * share : (j + 1) * share]
            for n, part in enumerate(pack_chunk(chunk)):
                out_ref[side, step * (per_run // 2) + j // 2, pl.ds(n * SUB, SUB), :] = part
        return carry

    lax.fori_loop(0, tiles // TILE_RUN, run, 0)


def delta_kernel(sum_ref, drift_ref, drift_norm_ref, out_ref):
    share = 6 * SUB
    channels = drift_ref.shape[2]
    total, gain_sum, shift_sum, frames = unpack_chunk(
        added([sum_ref[p] for p in range(sum_ref.shape[0])])
    )
    live_part = pltpu.roll(total, LANES - K, 1)
    norm_part = pltpu.roll(total, LANES - 2 * K, 1)
    kernel_sum = total - (shift_sum * live_part + gain_sum * norm_part) / frames
    start = lax.axis_index("dp") * share
    first = jnp.minimum(start // LANES, channels // LANES - 2)
    window = pl.ds(pl.multiple_of(first * LANES, LANES), 2 * LANES)
    drift = jnp.concatenate(
        [
            drift_ref[0, :, window].astype(jnp.float32),
            drift_norm_ref[0, :, window].astype(jnp.float32),
            jnp.zeros((LANES - K - 2, 2 * LANES), jnp.float32),
        ],
        axis=0,
    )
    drift = pltpu.roll(drift, lax.rem(2 * LANES - (start - first * LANES), 2 * LANES), 1)
    drift = drift[:, :LANES].T[:share]
    lane = lax.broadcasted_iota(jnp.int32, (share, LANES), 1)
    sums = jnp.where(lane < K, kernel_sum, jnp.where(lane == K, gain_sum, shift_sum))
    delta = (drift + (grad_factor_base / frames) * sums).astype(jnp.bfloat16).astype(jnp.float32)
    weighted = delta * frames
    block = share // 3
    lane = lane[:block]
    packed = jnp.broadcast_to(frames, (block, LANES))
    for b in range(3):
        piece = weighted[b * block : (b + 1) * block]
        moved = pltpu.roll(piece, b * K, 1) if b else piece
        packed = jnp.where((lane >= b * K) & (lane < (b + 1) * K), moved, packed)
        at = 3 * K + 2 * b
        moved = pltpu.roll(piece, at - K, 1)
        packed = jnp.where((lane >= at) & (lane < at + 2), moved, packed)
    for peer in range(out_ref.shape[0]):
        out_ref[peer] = packed


def average_kernel(sum_ref, kernel_ref, norm_ref):
    total = added([sum_ref[p] for p in range(sum_ref.shape[0])])
    block = total.shape[0]
    average = total / total[:, 3 * K + 6 : 3 * K + 7]
    average = jnp.concatenate([average, jnp.zeros((LANES - block, LANES), jnp.float32)], axis=0)
    turned = average.T
    for b in range(3):
        kernel_ref[:, b * block : (b + 1) * block] = turned[b * K : (b + 1) * K, :block]
        norm_ref[:, b * block : (b + 1) * block] = turned[3 * K + 2 * b : 3 * K + 2 * b + 2, :block]


VMEM_SPEC = pl.BlockSpec(memory_space=pltpu.VMEM)
HBM_SPEC = pl.BlockSpec(memory_space=pltpu.HBM)
PARAMS = pltpu.CompilerParams(vmem_limit_bytes=32 * 1024 * 1024)


def cost(flops):
    return pl.CostEstimate(flops=flops, bytes_accessed=0, transcendentals=0)


def conv_stage(frame_count, glu_in, kernel, cotangent):
    tiles = cotangent.shape[1] // LANES
    far = [
        pltpu.with_memory_space_constraint(x, pltpu.HBM)
        for x in (frame_count, glu_in, kernel, cotangent)
    ]
    return pl.pallas_call(
        conv_kernel,
        out_shape=(
            jax.ShapeDtypeStruct((tiles, 4, UTT * PADDED, LANES), jnp.float32),
            jax.ShapeDtypeStruct((tiles, ROWS, LANES), jnp.float32),
            jax.ShapeDtypeStruct((2 * tiles + SUB, LANES), jnp.float32),
            jax.ShapeDtypeStruct(cotangent.shape, cotangent.dtype),
            jax.ShapeDtypeStruct((tiles, K, LANES), jnp.float32),
            jax.ShapeDtypeStruct((ROWS, LANES), jnp.float32),
        ),
        in_specs=[HBM_SPEC] * 4,
        out_specs=(VMEM_SPEC,) * 6,
        scratch_shapes=[
            pltpu.SMEM((UTT,), jnp.int32),
            pltpu.VMEM(glu_in.shape, glu_in.dtype),
            pltpu.VMEM(kernel.shape, kernel.dtype),
            pltpu.VMEM((tiles, len(PRODUCTS), SUB, LANES), jnp.float32),
            pltpu.SemaphoreType.DMA((3,)),
            pltpu.SemaphoreType.DMA((len(CHUNKS), 2)),
        ],
        compiler_params=PARAMS,
        name="conv_stats",
    )(*far)


def pair_stage(stats, other, pairs):
    return pl.pallas_call(
        pair_kernel,
        out_shape=jax.ShapeDtypeStruct((pairs * (stats.shape[0] - SUB + 1), LANES), jnp.float32),
        in_specs=[VMEM_SPEC] * 2,
        out_specs=VMEM_SPEC,
        compiler_params=PARAMS,
        name="pair_stats",
    )(stats, other)


def back_stage(gathered, stats, cotangent, norm_params, fields, conv_out, live_sum, live, pairs):
    tiles = conv_out.shape[0]
    return pl.pallas_call(
        back_kernel,
        out_shape=jax.ShapeDtypeStruct((2, pairs, 5 * SUB, LANES), jnp.float32),
        in_specs=[VMEM_SPEC] * 8,
        out_specs=VMEM_SPEC,
        scratch_shapes=[
            pltpu.VMEM((2, tiles * LANES), jnp.float32),
            pltpu.VMEM((K * SUB, LANES), jnp.float32),
            pltpu.VMEM((K * SUB, LANES), jnp.float32),
        ],
        compiler_params=PARAMS,
        name="tap_sums",
    )(gathered, stats, cotangent, norm_params, fields, conv_out, live_sum, live)


def on_device(glu_in, cotangent, frame_count, kernel, norm_params, drift_kernel, drift_norm):
    n_dp = lax.axis_size("dp")
    n_group = lax.axis_size("group")
    pairs = n_dp // 2
    share = cotangent.shape[1] // n_dp
    swap = [(i, i ^ 1) for i in range(n_dp)]
    same_core = [[2 * p + core for p in range(pairs)] for core in range(2)]

    fields, conv_out, stats, cot_near, live_sum, live = conv_stage(
        frame_count, glu_in, kernel, cotangent
    )
    merged = pair_stage(stats, lax.ppermute(stats, "dp", swap), pairs)
    gathered = lax.all_to_all(
        merged.reshape(pairs, 1, -1), "dp", 0, 0, axis_index_groups=same_core
    ).reshape(merged.shape)

    both = back_stage(gathered, stats, cot_near, norm_params, fields, conv_out, live_sum, live, pairs)
    arrived = lax.ppermute(both[1], "dp", swap)
    tap_sums = lax.all_to_all(both[0] + arrived, "dp", 0, 0, axis_index_groups=same_core)

    weighted = pl.pallas_call(
        delta_kernel,
        out_shape=jax.ShapeDtypeStruct((n_group, share // 3, LANES), jnp.float32),
        in_specs=[VMEM_SPEC] * 3,
        out_specs=VMEM_SPEC,
        compiler_params=PARAMS,
        name="group_delta",
    )(tap_sums, drift_kernel, drift_norm)
    weighted = lax.all_to_all(weighted, "group", 0, 0)

    return pl.pallas_call(
        average_kernel,
        out_shape=(
            jax.ShapeDtypeStruct((K, share), jnp.float32),
            jax.ShapeDtypeStruct((2, share), jnp.float32),
        ),
        in_specs=[VMEM_SPEC],
        out_specs=(VMEM_SPEC, VMEM_SPEC),
        compiler_params=PARAMS,
        name="group_average",
    )(weighted)


def solution(mesh):
    placed = (
        P(("dp", "group"), None),
        P(("dp", "group"), None),
        P(("dp", "group")),
        P("group", None, None),
        P("group", None, None),
        P("group", None, None),
        P("group", None, None),
    )
    return jax.shard_map(
        on_device,
        mesh=mesh,
        in_specs=placed,
        out_specs=(P(None, "dp"), P(None, "dp")),
        check_vma=False,
    )
```

```python
import functools
import operator

import jax
import jax.numpy as jnp
from jax import lax
from jax.experimental import pallas as pl
from jax.experimental.pallas import tpu as pltpu
from jax.sharding import PartitionSpec as P

K = 32
HALF = K // 2
SUB = 8
LANES = 128
SLOT = 128
UTT = 2
ROWS = UTT * SLOT
PADDED = HALF + SLOT + HALF
SHARE = 48
RUNS = 2
PARTS = 4
COT_AT = ROWS
LIVE_AT = 2 * ROWS
COUNT_AT = LIVE_AT + K
PACK_ROWS = COUNT_AT + SUB
TILE_RUN = 3

grad_factor_base = 128.0
eps_norm = 1e-05


def lane_tile(i):
    return pl.ds(pl.multiple_of(i * LANES, LANES), LANES)


def peer_rows(row, peers, tiles):
    return pl.ds(row, peers, stride=2 * tiles + 1)


WINDOWS = ((0, 3), (1, 4), (3, 3))


def share_picker(m, core):
    first, count = WINDOWS[m]
    column = lax.broadcasted_iota(jnp.int32, (1, 2 * LANES), 1)
    mine = column < LANES
    at = m * LANES + jnp.where(mine, column, column - LANES)
    shares = added([jnp.where(at >= n * SHARE, 1, 0) for n in range(1, TILE_RUN * LANES // SHARE)])
    source = at + SHARE * (shares + jnp.where(mine, core, 1 - core)) - first * LANES
    row = lax.broadcasted_iota(jnp.int32, (count * LANES, 2 * LANES), 0)
    return jnp.where(row == source, 1.0, 0.0).astype(jnp.bfloat16)


def picked(block, picker):
    return jnp.dot(block, picker, preferred_element_type=jnp.float32)


def live_rows(count):
    return lax.broadcasted_iota(jnp.int32, (SLOT, LANES), 0) < count


def added(terms):
    return functools.reduce(operator.add, terms)


def fold_rows(field):
    return jnp.sum(field.reshape(field.shape[0] // SUB, SUB, LANES), axis=0)


def scan_rows(field, upward):
    row = lax.broadcasted_iota(jnp.int32, field.shape, 0)
    step = 1
    while step < HALF:
        if upward:
            moved = jnp.where(row < HALF - step, pltpu.roll(field, HALF - step, 0), 0.0)
        else:
            moved = jnp.where(row >= step, pltpu.roll(field, step, 0), 0.0)
        field = field + moved
        step *= 2
    return field


PLAIN, NEXT, SECOND, BOTH = range(4)
PRODUCTS = (
    (PLAIN, 3),
    (SECOND, 1),
    (SECOND, 3),
    (NEXT, 2),
    (BOTH, 0),
    (BOTH, 2),
    (NEXT, 3),
    (BOTH, 1),
    (BOTH, 3),
)
COMBOS = ((0, 1, 2, 3), (0, 1), (2, 3), (0, 2), (0,), (2,), (1, 3), (1,), (3,))


def combine(parts):
    low = parts[0] + parts[1]
    high = parts[0] - parts[2]
    return (
        low + (parts[3] + parts[4]),
        low - (parts[6] + parts[7]),
        high + (parts[3] - parts[5]),
        high - (parts[6] - parts[8]),
    )


def fields_at(field_ref, i, row, product):
    kind, block = product
    return [
        field_ref[i, kind, pl.ds(row + SUB * (4 * m + block), SUB), :] for m in range(SLOT // SUB // 4)
    ]


def gate_kernel(
    count_hbm,
    glu_hbm,
    kernel_hbm,
    param_hbm,
    cot_hbm,
    own_ref,
    other_ref,
    taps_ref,
    par_ref,
    count_ref,
    glu_ref,
    kernel_ref,
    param_ref,
    cot_ref,
    small_sems,
    run_sems,
):
    channels = cot_ref.shape[1]
    width = channels // RUNS
    core = lax.rem(lax.axis_index("dp"), 2)
    small = [
        pltpu.make_async_copy(far, close, small_sems.at[n])
        for n, (far, close) in enumerate(
            ((count_hbm, count_ref), (kernel_hbm, kernel_ref), (param_hbm, param_ref))
        )
    ]
    copies = []
    for g in range(RUNS):
        for n, (far, close, at) in enumerate(
            (
                (glu_hbm, glu_ref, g * width),
                (glu_hbm, glu_ref, channels + g * width),
                (cot_hbm, cot_ref, g * width),
            )
        ):
            columns = pl.ds(at, width)
            copies.append(
                pltpu.make_async_copy(far.at[:, columns], close.at[:, columns], run_sems.at[g, n])
            )
    for copy in small + copies:
        copy.start()
    pickers = [share_picker(m, core) for m in range(TILE_RUN)]
    for copy in small:
        copy.wait()
    counts = [count_ref[u] for u in range(UTT)]
    lives = [jnp.where(live_rows(count), 1.0, 0.0) for count in counts]
    row = lax.broadcasted_iota(jnp.int32, (SUB, LANES), 0)
    count_rows = jnp.where(row == 0, counts[0], counts[1]).astype(jnp.float32)
    for g in range(RUNS):
        for copy in copies[3 * g : 3 * g + 3]:
            copy.wait()
        for m, (first, count) in enumerate(WINDOWS):
            t = g * TILE_RUN + m
            start = g * width + first * LANES
            span = count * LANES
            both = pickers[m]
            gated = picked(glu_ref[:, start : start + span], both) * jax.nn.sigmoid(
                picked(glu_ref[:, channels + start : channels + start + span], both)
            )
            cot = picked(cot_ref[:, start : start + span], both)
            small_rows = jnp.concatenate(
                [
                    kernel_ref[0, :, start : start + span].astype(jnp.float32),
                    param_ref[0, :, start : start + span].astype(jnp.float32),
                    jnp.zeros((SUB - 2, span), jnp.float32),
                ],
                axis=0,
            ).astype(jnp.bfloat16)
            small_rows = picked(small_rows, both[:, :LANES])
            rows = [small_rows[SUB * j : SUB * (j + 1)] for j in range(K // SUB)]
            for n, combo in enumerate(COMBOS):
                taps_ref[t, n] = added([rows[j] for j in combo])
            par_ref[t] = small_rows[K:]
            for side, ref in enumerate((own_ref, other_ref)):
                lanes = slice(side * LANES, (side + 1) * LANES)
                heads = []
                tails = []
                sums = []
                for u in range(UTT):
                    part = gated[u * SLOT : (u + 1) * SLOT, lanes] * lives[u]
                    ref[t, pl.ds(u * SLOT, SLOT), :] = part
                    sums.append(fold_rows(part))
                    heads.append(part[:HALF])
                    tails.append(ref[t, pl.ds(u * SLOT + counts[u] - HALF, HALF), :])
                head = added(heads)
                ref[t, pl.ds(COT_AT, ROWS), :] = cot[:, lanes]
                ref[t, pl.ds(LIVE_AT, K), :] = jnp.sum(
                    added(sums), axis=0, keepdims=True
                ) - jnp.concatenate(
                    [scan_rows(added(tails), True), scan_rows(head, False) - head], axis=0
                )
                ref[t, pl.ds(COUNT_AT, SUB), :] = count_rows


def conv_kernel(own_ref, other_ref, taps_ref, field_ref, conv_ref, live_ref, send_ref):
    tiles = conv_ref.shape[0]
    rows_each = 2 * tiles + 1
    peers = send_ref.shape[0] // rows_each
    sources = (own_ref, own_ref, other_ref, other_ref)
    counts = [sources[u][0, pl.ds(COUNT_AT + u % UTT, 1), :] for u in range(PARTS)]
    local_frames = added(counts)
    position = lax.broadcasted_iota(jnp.int32, (SLOT, LANES), 0).astype(jnp.float32)
    for u in range(PARTS):
        live_ref[pl.ds(u * SLOT, SLOT), :] = jnp.where(position < counts[u], 1.0, 0.0)
    send_ref[peer_rows(2 * tiles, peers, tiles), :] = jnp.broadcast_to(local_frames, (peers, LANES))

    def tile(i, carry):
        edge = jnp.zeros((HALF, LANES), jnp.float32)
        total = jnp.zeros((SUB, LANES), jnp.float32)
        for u in range(PARTS):
            base = u * PADDED
            field = sources[u][i, pl.ds(u % UTT * SLOT, SLOT), :]
            field = jnp.concatenate([edge, field, edge], axis=0)
            close = field[: PADDED - SUB] - field[SUB:]
            field_ref[i, PLAIN, pl.ds(base, PADDED), :] = field
            field_ref[i, NEXT, pl.ds(base, PADDED - SUB), :] = close
            field_ref[i, SECOND, pl.ds(base, PADDED - 2 * SUB), :] = (
                field[: PADDED - 2 * SUB] - field[2 * SUB :]
            )
            field_ref[i, BOTH, pl.ds(base, PADDED - 3 * SUB), :] = (
                close[: PADDED - 3 * SUB] - close[2 * SUB :]
            )
        for u in range(PARTS):
            base = u * PADDED
            sums = [None] * (4 * len(PRODUCTS))
            for first in range(SUB):
                for n, product in enumerate(PRODUCTS):
                    tap = taps_ref[i, n, pl.ds(first, 1), :]
                    for m, field in enumerate(fields_at(field_ref, i, base + first, product)):
                        term = field * tap
                        sums[4 * n + m] = term if first == 0 else sums[4 * n + m] + term
            for m in range(SLOT // SUB // 4):
                for q, out in enumerate(combine(sums[m::4])):
                    at = pl.ds(u * SLOT + SUB * (4 * m + q), SUB)
                    conv_ref[i, at, :] = out
                    total = total + out * live_ref[at, :]
        local_mean = jnp.sum(total, axis=0, keepdims=True) / local_frames
        spread = jnp.zeros((SUB, LANES), jnp.float32)
        for u in range(PARTS):
            rows = pl.ds(u * SLOT, SLOT)
            centered = (conv_ref[i, rows, :] - local_mean) * live_ref[rows, :]
            spread = spread + fold_rows(centered * centered)
        spread = jnp.sum(spread, axis=0, keepdims=True)
        send_ref[peer_rows(i, peers, tiles), :] = jnp.broadcast_to(local_mean, (peers, LANES))
        send_ref[peer_rows(i + tiles, peers, tiles), :] = jnp.broadcast_to(spread, (peers, LANES))
        return carry

    lax.fori_loop(0, tiles, tile, 0)


def store_taps(tap_ref, field_ref, i, u, source):
    blocks = [source[SUB * q : SUB * (q + 1)] for q in range(SLOT // SUB)]
    mixes = [
        [added([blocks[4 * m + q] for q in combo]) for m in range(SLOT // SUB // 4)]
        for combo in COMBOS
    ]
    for first in range(SUB):
        parts = []
        for mix, product in zip(mixes, PRODUCTS):
            fields = fields_at(field_ref, i, u * PADDED + first, product)
            parts.append(added([x * field for x, field in zip(mix, fields)]))
        for j, out in enumerate(combine(parts)):
            at = pl.ds(SUB * (first + SUB * j), SUB)
            tap_ref[at, :] = out if u == 0 else tap_ref[at, :] + out


def load_taps(tap_ref):
    return added([tap_ref[pl.ds(row, K, stride=SUB), :] for row in range(SUB)])


def lane_in(low, high):
    lane = lax.broadcasted_iota(jnp.int32, (SUB, LANES), 1)
    return (lane >= low) & (lane < high)


def pack_chunk(chunk):
    blocks = [chunk[SUB * b : SUB * (b + 1)] for b in range(6)]
    last = pltpu.roll(blocks[5], 3 * K, 1)
    moved = [pltpu.roll(blocks[4], (3 - n) * K, 1) for n in range(3)] + [last]
    packed = [jnp.where(lane_in(0, 3 * K), blocks[n], moved[n]) for n in range(4)]
    for b in range(6):
        extra = pltpu.roll(blocks[b], LANES - K + 2 * b, 1)
        last = jnp.where(lane_in(2 * K + 2 * b, 2 * K + 2 * b + 3), extra, last)
    return packed + [last]


def unpack_chunk(packed):
    parts = [packed[SUB * n : SUB * (n + 1)] for n in range(5)]
    four = pltpu.roll(parts[0], K, 1)
    four = jnp.where(lane_in(K, 2 * K), pltpu.roll(parts[1], 2 * K, 1), four)
    four = jnp.where(lane_in(2 * K, 3 * K), pltpu.roll(parts[2], 3 * K, 1), four)
    five = jnp.where(lane_in(0, K), pltpu.roll(parts[3], K, 1), pltpu.roll(parts[4], K, 1))
    sums = jnp.concatenate(parts[:4] + [four, five], axis=0)
    at = [2 * K + 2 * b for b in range(6)]
    gain_sum = jnp.concatenate([parts[4][:, n : n + 1] for n in at], axis=0)
    shift_sum = jnp.concatenate([parts[4][:, n + 1 : n + 2] for n in at], axis=0)
    return sums, gain_sum, shift_sum, parts[4][:1, at[5] + 2 : at[5] + 3]


def back_kernel(
    stat_ref,
    own_ref,
    other_ref,
    par_ref,
    field_ref,
    conv_ref,
    live_ref,
    out_ref,
    up_ref,
    norm_ref,
):
    tiles = conv_ref.shape[0]
    pairs = out_ref.shape[0]
    per_run = TILE_RUN * LANES // SHARE
    sources = (own_ref, own_ref, other_ref, other_ref)
    local_frames = added([sources[u][0, pl.ds(COUNT_AT + u % UTT, 1), :] for u in range(PARTS)])
    counts = stat_ref[peer_rows(2 * tiles, pairs, tiles), :]
    frames = jnp.sum(counts, axis=0, keepdims=True)
    row = lax.broadcasted_iota(jnp.int32, (SUB, LANES), 0)
    rest = jnp.zeros((K - SUB, LANES), jnp.float32)

    def tile(i):
        means = stat_ref[peer_rows(i, pairs, tiles), :]
        mean_row = jnp.sum(counts * means, axis=0, keepdims=True) / frames
        apart = means - mean_row
        spread = stat_ref[peer_rows(i + tiles, pairs, tiles), :] + counts * apart * apart
        inv_row = lax.rsqrt(jnp.sum(spread, axis=0, keepdims=True) / frames + eps_norm)
        gain_row = par_ref[i, pl.ds(0, 1), :]
        shift_row = par_ref[i, pl.ds(1, 1), :]
        gain_sum = jnp.zeros((SUB, LANES), jnp.float32)
        shift_sum = jnp.zeros((SUB, LANES), jnp.float32)
        for u in range(PARTS):
            rows = pl.ds(u * SLOT, SLOT)
            live = live_ref[rows, :]
            normed = (conv_ref[i, rows, :] - mean_row) * inv_row
            norm_out = gain_row * normed + shift_row
            sig = jax.nn.sigmoid(norm_out)
            slope = sig * (1.0 + norm_out * (1.0 - sig))
            upstream = sources[u][i, pl.ds(COT_AT + u % UTT * SLOT, SLOT), :] * slope * live
            normed = normed * live
            gain_sum = gain_sum + fold_rows(upstream * normed)
            shift_sum = shift_sum + fold_rows(upstream)
            store_taps(up_ref, field_ref, i, u, upstream)
            store_taps(norm_ref, field_ref, i, u, normed)
        scale = gain_row * inv_row
        extra = jnp.where(row == 0, jnp.sum(gain_sum, axis=0, keepdims=True), local_frames)
        extra = jnp.where(row == 1, jnp.sum(shift_sum, axis=0, keepdims=True), extra)
        live_sum = own_ref[i, pl.ds(LIVE_AT, K), :] + other_ref[i, pl.ds(LIVE_AT, K), :]
        block = jnp.concatenate(
            [load_taps(up_ref) * scale, live_sum * scale, load_taps(norm_ref) * scale, extra, rest],
            axis=0,
        )
        return block.T

    def run(step, carry):
        turned = jnp.concatenate([tile(step * TILE_RUN + n) for n in range(TILE_RUN)], axis=0)
        for j in range(per_run):
            for n, part in enumerate(pack_chunk(turned[j * SHARE : (j + 1) * SHARE])):
                out_ref[step * per_run + j, pl.ds(n * SUB, SUB), :] = part
        return carry

    lax.fori_loop(0, tiles // TILE_RUN, run, 0)


def delta_kernel(sum_ref, drift_ref, drift_norm_ref, out_ref):
    share = SHARE
    channels = drift_ref.shape[2]
    total, gain_sum, shift_sum, frames = unpack_chunk(
        added([sum_ref[p] for p in range(sum_ref.shape[0])])
    )
    live_part = pltpu.roll(total, LANES - K, 1)
    norm_part = pltpu.roll(total, LANES - 2 * K, 1)
    kernel_sum = total - (shift_sum * live_part + gain_sum * norm_part) / frames
    start = lax.axis_index("dp") * share
    first = jnp.minimum(start // LANES, channels // LANES - 2)
    window = pl.ds(pl.multiple_of(first * LANES, LANES), 2 * LANES)
    drift = jnp.concatenate(
        [
            drift_ref[0, :, window].astype(jnp.float32),
            drift_norm_ref[0, :, window].astype(jnp.float32),
            jnp.zeros((LANES - K - 2, 2 * LANES), jnp.float32),
        ],
        axis=0,
    )
    drift = pltpu.roll(drift, lax.rem(2 * LANES - (start - first * LANES), 2 * LANES), 1)
    drift = drift[:, :LANES].T[:share]
    lane = lax.broadcasted_iota(jnp.int32, (share, LANES), 1)
    sums = jnp.where(lane < K, kernel_sum, jnp.where(lane == K, gain_sum, shift_sum))
    delta = (drift + (grad_factor_base / frames) * sums).astype(jnp.bfloat16).astype(jnp.float32)
    weighted = delta * frames
    block = share // 3
    lane = lane[:block]
    packed = jnp.broadcast_to(frames, (block, LANES))
    for b in range(3):
        piece = weighted[b * block : (b + 1) * block]
        moved = pltpu.roll(piece, b * K, 1) if b else piece
        packed = jnp.where((lane >= b * K) & (lane < (b + 1) * K), moved, packed)
        at = 3 * K + 2 * b
        moved = pltpu.roll(piece, at - K, 1)
        packed = jnp.where((lane >= at) & (lane < at + 2), moved, packed)
    for peer in range(out_ref.shape[0]):
        out_ref[peer] = packed


def average_kernel(sum_ref, kernel_ref, norm_ref):
    total = added([sum_ref[p] for p in range(sum_ref.shape[0])])
    block = total.shape[0]
    average = total / total[:, 3 * K + 6 : 3 * K + 7]
    average = jnp.concatenate([average, jnp.zeros((LANES - block, LANES), jnp.float32)], axis=0)
    turned = average.T
    for b in range(3):
        kernel_ref[:, b * block : (b + 1) * block] = turned[b * K : (b + 1) * K, :block]
        norm_ref[:, b * block : (b + 1) * block] = turned[3 * K + 2 * b : 3 * K + 2 * b + 2, :block]


VMEM_SPEC = pl.BlockSpec(memory_space=pltpu.VMEM)
HBM_SPEC = pl.BlockSpec(memory_space=pltpu.HBM)
PARAMS = pltpu.CompilerParams(vmem_limit_bytes=32 * 1024 * 1024)


def cost(flops):
    return pl.CostEstimate(flops=flops, bytes_accessed=0, transcendentals=0)


def gate_stage(frame_count, glu_in, kernel, norm_params, cotangent):
    tiles = cotangent.shape[1] // LANES // 2
    far = [
        pltpu.with_memory_space_constraint(x, pltpu.HBM)
        for x in (frame_count, glu_in, kernel, norm_params, cotangent)
    ]
    return pl.pallas_call(
        gate_kernel,
        out_shape=(
            jax.ShapeDtypeStruct((tiles, PACK_ROWS, LANES), jnp.float32),
            jax.ShapeDtypeStruct((tiles, PACK_ROWS, LANES), jnp.float32),
            jax.ShapeDtypeStruct((tiles, len(PRODUCTS), SUB, LANES), jnp.float32),
            jax.ShapeDtypeStruct((tiles, SUB, LANES), jnp.float32),
        ),
        in_specs=[HBM_SPEC] * 5,
        out_specs=(VMEM_SPEC,) * 4,
        scratch_shapes=[
            pltpu.SMEM((UTT,), jnp.int32),
            pltpu.VMEM(glu_in.shape, glu_in.dtype),
            pltpu.VMEM(kernel.shape, kernel.dtype),
            pltpu.VMEM(norm_params.shape, norm_params.dtype),
            pltpu.VMEM(cotangent.shape, cotangent.dtype),
            pltpu.SemaphoreType.DMA((3,)),
            pltpu.SemaphoreType.DMA((RUNS, 3)),
        ],
        compiler_params=PARAMS,
        name="gate_shares",
    )(*far)


def conv_stage(own, other, taps, peers):
    tiles = own.shape[0]
    return pl.pallas_call(
        conv_kernel,
        out_shape=(
            jax.ShapeDtypeStruct((tiles, 4, PARTS * PADDED, LANES), jnp.float32),
            jax.ShapeDtypeStruct((tiles, PARTS * SLOT, LANES), jnp.float32),
            jax.ShapeDtypeStruct((PARTS * SLOT, LANES), jnp.float32),
            jax.ShapeDtypeStruct((peers * (2 * tiles + 1), LANES), jnp.float32),
        ),
        in_specs=[VMEM_SPEC] * 3,
        out_specs=(VMEM_SPEC,) * 4,
        compiler_params=PARAMS,
        name="conv_stats",
    )(own, other, taps)


def back_stage(gathered, own, other, norm_rows, fields, conv_out, live, peers):
    return pl.pallas_call(
        back_kernel,
        out_shape=jax.ShapeDtypeStruct((peers, 5 * SUB, LANES), jnp.float32),
        in_specs=[VMEM_SPEC] * 7,
        out_specs=VMEM_SPEC,
        scratch_shapes=[
            pltpu.VMEM((K * SUB, LANES), jnp.float32),
            pltpu.VMEM((K * SUB, LANES), jnp.float32),
        ],
        compiler_params=PARAMS,
        name="tap_sums",
    )(gathered, own, other, norm_rows, fields, conv_out, live)


def on_device(glu_in, cotangent, frame_count, kernel, norm_params, drift_kernel, drift_norm):
    n_dp = lax.axis_size("dp")
    n_group = lax.axis_size("group")
    pairs = n_dp // 2
    swap = [(i, i ^ 1) for i in range(n_dp)]
    same_core = [[2 * p + core for p in range(pairs)] for core in range(2)]

    own, other, taps, norm_rows = gate_stage(frame_count, glu_in, kernel, norm_params, cotangent)
    other = lax.ppermute(other, "dp", swap)
    fields, conv_out, live, stats = conv_stage(own, other, taps, pairs)
    gathered = lax.all_to_all(
        stats.reshape(pairs, 1, -1), "dp", 0, 0, axis_index_groups=same_core
    ).reshape(stats.shape)

    tap_sums = back_stage(gathered, own, other, norm_rows, fields, conv_out, live, pairs)
    tap_sums = lax.all_to_all(tap_sums, "dp", 0, 0, axis_index_groups=same_core)

    weighted = pl.pallas_call(
        delta_kernel,
        out_shape=jax.ShapeDtypeStruct((n_group, SHARE // 3, LANES), jnp.float32),
        in_specs=[VMEM_SPEC] * 3,
        out_specs=VMEM_SPEC,
        compiler_params=PARAMS,
        name="group_delta",
    )(tap_sums, drift_kernel, drift_norm)
    weighted = lax.all_to_all(weighted, "group", 0, 0)

    return pl.pallas_call(
        average_kernel,
        out_shape=(
            jax.ShapeDtypeStruct((K, SHARE), jnp.float32),
            jax.ShapeDtypeStruct((2, SHARE), jnp.float32),
        ),
        in_specs=[VMEM_SPEC],
        out_specs=(VMEM_SPEC, VMEM_SPEC),
        compiler_params=PARAMS,
        name="group_average",
    )(weighted)


def solution(mesh):
    placed = (
        P(("dp", "group"), None),
        P(("dp", "group"), None),
        P(("dp", "group")),
        P("group", None, None),
        P("group", None, None),
        P("group", None, None),
        P("group", None, None),
    )
    return jax.shard_map(
        on_device,
        mesh=mesh,
        in_specs=placed,
        out_specs=(P(None, "dp"), P(None, "dp")),
        check_vma=False,
    )
```

```python
import functools
import operator

import jax
import jax.numpy as jnp
from jax import lax
from jax.experimental import pallas as pl
from jax.experimental.pallas import tpu as pltpu
from jax.sharding import PartitionSpec as P

K = 32
HALF = K // 2
SUB = 8
LANES = 128
SLOT = 128
UTT = 2
ROWS = UTT * SLOT
PADDED = HALF + SLOT + HALF
SHARE = 48
RUNS = 2
UNROLL = 1
COT_AT = ROWS
LIVE_AT = 2 * ROWS
COUNT_AT = LIVE_AT + K
PACK_ROWS = COUNT_AT + SUB
TILE_RUN = 3

grad_factor_base = 128.0
eps_norm = 1e-05


def lane_tile(i):
    return pl.ds(pl.multiple_of(i * LANES, LANES), LANES)


def peer_rows(row, peers, tiles):
    return pl.ds(row, peers, stride=2 * tiles + 1)


WINDOWS = ((0, 3), (1, 4), (3, 3))


def share_picker(m, core):
    first, count = WINDOWS[m]
    column = lax.broadcasted_iota(jnp.int32, (1, 2 * LANES), 1)
    mine = column < LANES
    at = m * LANES + jnp.where(mine, column, column - LANES)
    shares = added([jnp.where(at >= n * SHARE, 1, 0) for n in range(1, TILE_RUN * LANES // SHARE)])
    source = at + SHARE * (shares + jnp.where(mine, core, 1 - core)) - first * LANES
    row = lax.broadcasted_iota(jnp.int32, (count * LANES, 2 * LANES), 0)
    return jnp.where(row == source, 1.0, 0.0).astype(jnp.bfloat16)


def picked(block, picker):
    return jnp.dot(block, picker, preferred_element_type=jnp.float32)


def live_rows(count):
    return lax.broadcasted_iota(jnp.int32, (SLOT, LANES), 0) < count


def added(terms):
    return functools.reduce(operator.add, terms)


def fold_rows(field):
    return jnp.sum(field.reshape(field.shape[0] // SUB, SUB, LANES), axis=0)


def scan_rows(field, upward):
    row = lax.broadcasted_iota(jnp.int32, field.shape, 0)
    step = 1
    while step < HALF:
        if upward:
            moved = jnp.where(row < HALF - step, pltpu.roll(field, HALF - step, 0), 0.0)
        else:
            moved = jnp.where(row >= step, pltpu.roll(field, step, 0), 0.0)
        field = field + moved
        step *= 2
    return field


PLAIN, NEXT, SECOND, BOTH = range(4)
PRODUCTS = (
    (PLAIN, 3),
    (SECOND, 1),
    (SECOND, 3),
    (NEXT, 2),
    (BOTH, 0),
    (BOTH, 2),
    (NEXT, 3),
    (BOTH, 1),
    (BOTH, 3),
)
COMBOS = ((0, 1, 2, 3), (0, 1), (2, 3), (0, 2), (0,), (2,), (1, 3), (1,), (3,))


def combine(parts):
    low = parts[0] + parts[1]
    high = parts[0] - parts[2]
    return (
        low + (parts[3] + parts[4]),
        low - (parts[6] + parts[7]),
        high + (parts[3] - parts[5]),
        high - (parts[6] - parts[8]),
    )


def fields_at(field_ref, i, row, product):
    kind, block = product
    return [
        field_ref[i, kind, pl.ds(row + SUB * (4 * m + block), SUB), :] for m in range(SLOT // SUB // 4)
    ]


def gate_kernel(
    count_hbm,
    glu_hbm,
    kernel_hbm,
    param_hbm,
    cot_hbm,
    own_ref,
    other_ref,
    taps_ref,
    par_ref,
    count_ref,
    glu_ref,
    kernel_ref,
    param_ref,
    cot_ref,
    small_sems,
    run_sems,
):
    channels = cot_ref.shape[1]
    width = channels // RUNS
    core = lax.rem(lax.axis_index("dp"), 2)
    small = [
        pltpu.make_async_copy(far, close, small_sems.at[n])
        for n, (far, close) in enumerate(
            ((count_hbm, count_ref), (kernel_hbm, kernel_ref), (param_hbm, param_ref))
        )
    ]
    copies = []
    for g in range(RUNS):
        for n, (far, close, at) in enumerate(
            (
                (glu_hbm, glu_ref, g * width),
                (glu_hbm, glu_ref, channels + g * width),
                (cot_hbm, cot_ref, g * width),
            )
        ):
            columns = pl.ds(at, width)
            copies.append(
                pltpu.make_async_copy(far.at[:, columns], close.at[:, columns], run_sems.at[g, n])
            )
    for copy in small + copies:
        copy.start()
    pickers = [share_picker(m, core) for m in range(TILE_RUN)]
    for copy in small:
        copy.wait()
    counts = [count_ref[u] for u in range(UTT)]
    lives = [jnp.where(live_rows(count), 1.0, 0.0) for count in counts]
    row = lax.broadcasted_iota(jnp.int32, (SUB, LANES), 0)
    count_rows = jnp.where(row == 0, counts[0], counts[1]).astype(jnp.float32)
    for g in range(RUNS):
        for copy in copies[3 * g : 3 * g + 3]:
            copy.wait()
        for m, (first, count) in enumerate(WINDOWS):
            t = g * TILE_RUN + m
            start = g * width + first * LANES
            span = count * LANES
            both = pickers[m]
            gated = picked(glu_ref[:, start : start + span], both) * jax.nn.sigmoid(
                picked(glu_ref[:, channels + start : channels + start + span], both)
            )
            cot = picked(cot_ref[:, start : start + span], both)
            small_rows = jnp.concatenate(
                [
                    kernel_ref[0, :, start : start + span].astype(jnp.float32),
                    param_ref[0, :, start : start + span].astype(jnp.float32),
                    jnp.zeros((SUB - 2, span), jnp.float32),
                ],
                axis=0,
            ).astype(jnp.bfloat16)
            small_rows = picked(small_rows, both[:, :LANES])
            rows = [small_rows[SUB * j : SUB * (j + 1)] for j in range(K // SUB)]
            for n, combo in enumerate(COMBOS):
                taps_ref[t, n] = added([rows[j] for j in combo])
            par_ref[t] = small_rows[K:]
            for side, ref in enumerate((own_ref, other_ref)):
                lanes = slice(side * LANES, (side + 1) * LANES)
                heads = []
                tails = []
                sums = []
                for u in range(UTT):
                    part = gated[u * SLOT : (u + 1) * SLOT, lanes] * lives[u]
                    ref[t, pl.ds(u * SLOT, SLOT), :] = part
                    sums.append(fold_rows(part))
                    heads.append(part[:HALF])
                    tails.append(ref[t, pl.ds(u * SLOT + counts[u] - HALF, HALF), :])
                head = added(heads)
                ref[t, pl.ds(COT_AT, ROWS), :] = cot[:, lanes]
                ref[t, pl.ds(LIVE_AT, K), :] = jnp.sum(
                    added(sums), axis=0, keepdims=True
                ) - jnp.concatenate(
                    [scan_rows(added(tails), True), scan_rows(head, False) - head], axis=0
                )
                ref[t, pl.ds(COUNT_AT, SUB), :] = count_rows


def convolve(i, source_ref, taps_ref, live_ref, field_ref, conv_ref):
    edge = jnp.zeros((HALF, LANES), jnp.float32)
    total = jnp.zeros((SUB, LANES), jnp.float32)
    for u in range(UTT):
        base = u * PADDED
        field = source_ref[i, pl.ds(u * SLOT, SLOT), :]
        field = jnp.concatenate([edge, field, edge], axis=0)
        close = field[: PADDED - SUB] - field[SUB:]
        field_ref[i, PLAIN, pl.ds(base, PADDED), :] = field
        field_ref[i, NEXT, pl.ds(base, PADDED - SUB), :] = close
        field_ref[i, SECOND, pl.ds(base, PADDED - 2 * SUB), :] = (
            field[: PADDED - 2 * SUB] - field[2 * SUB :]
        )
        field_ref[i, BOTH, pl.ds(base, PADDED - 3 * SUB), :] = (
            close[: PADDED - 3 * SUB] - close[2 * SUB :]
        )
    for u in range(UTT):
        base = u * PADDED
        sums = [None] * (4 * len(PRODUCTS))
        for first in range(SUB):
            for n, product in enumerate(PRODUCTS):
                tap = taps_ref[i, n, pl.ds(first, 1), :]
                for m, field in enumerate(fields_at(field_ref, i, base + first, product)):
                    term = field * tap
                    sums[4 * n + m] = term if first == 0 else sums[4 * n + m] + term
        for m in range(SLOT // SUB // 4):
            for q, out in enumerate(combine(sums[m::4])):
                at = pl.ds(u * SLOT + SUB * (4 * m + q), SUB)
                conv_ref[i, at, :] = out
                total = total + out * live_ref[at, :]
    return total


def live_masks(source_ref, live_ref):
    position = lax.broadcasted_iota(jnp.int32, (SLOT, LANES), 0).astype(jnp.float32)
    counts = [source_ref[0, pl.ds(COUNT_AT + u, 1), :] for u in range(UTT)]
    for u in range(UTT):
        live_ref[pl.ds(u * SLOT, SLOT), :] = jnp.where(position < counts[u], 1.0, 0.0)
    return added(counts)


def own_conv_kernel(own_ref, taps_ref, field_ref, conv_ref, live_ref, total_ref):
    live_masks(own_ref, live_ref)

    def tile(i, carry):
        total_ref[i] = convolve(i, own_ref, taps_ref, live_ref, field_ref, conv_ref)
        return carry

    lax.fori_loop(0, conv_ref.shape[0], tile, 0, unroll=UNROLL)


def conv_kernel(
    own_ref,
    other_ref,
    taps_ref,
    own_conv_ref,
    own_live_ref,
    own_total_ref,
    field_ref,
    conv_ref,
    live_ref,
    send_ref,
):
    tiles = conv_ref.shape[0]
    peers = send_ref.shape[0] // (2 * tiles + 1)
    own_counts = [own_ref[0, pl.ds(COUNT_AT + u, 1), :] for u in range(UTT)]
    local_frames = live_masks(other_ref, live_ref) + added(own_counts)
    send_ref[peer_rows(2 * tiles, peers, tiles), :] = jnp.broadcast_to(local_frames, (peers, LANES))

    def tile(i, carry):
        total = own_total_ref[i] + convolve(i, other_ref, taps_ref, live_ref, field_ref, conv_ref)
        local_mean = jnp.sum(total, axis=0, keepdims=True) / local_frames
        spread = jnp.zeros((SUB, LANES), jnp.float32)
        for values, live in ((own_conv_ref, own_live_ref), (conv_ref, live_ref)):
            centered = (values[i] - local_mean) * live[...]
            spread = spread + fold_rows(centered * centered)
        spread = jnp.sum(spread, axis=0, keepdims=True)
        send_ref[peer_rows(i, peers, tiles), :] = jnp.broadcast_to(local_mean, (peers, LANES))
        send_ref[peer_rows(i + tiles, peers, tiles), :] = jnp.broadcast_to(spread, (peers, LANES))
        return carry

    lax.fori_loop(0, tiles, tile, 0, unroll=UNROLL)


def store_taps(tap_ref, field_ref, i, u, source, first_part):
    blocks = [source[SUB * q : SUB * (q + 1)] for q in range(SLOT // SUB)]
    mixes = [
        [added([blocks[4 * m + q] for q in combo]) for m in range(SLOT // SUB // 4)]
        for combo in COMBOS
    ]
    for first in range(SUB):
        parts = []
        for mix, product in zip(mixes, PRODUCTS):
            fields = fields_at(field_ref, i, u * PADDED + first, product)
            parts.append(added([x * field for x, field in zip(mix, fields)]))
        for j, out in enumerate(combine(parts)):
            at = pl.ds(SUB * (first + SUB * j), SUB)
            tap_ref[at, :] = out if first_part else tap_ref[at, :] + out


def load_taps(tap_ref):
    return added([tap_ref[pl.ds(row, K, stride=SUB), :] for row in range(SUB)])


def lane_in(low, high):
    lane = lax.broadcasted_iota(jnp.int32, (SUB, LANES), 1)
    return (lane >= low) & (lane < high)


def pack_chunk(chunk):
    blocks = [chunk[SUB * b : SUB * (b + 1)] for b in range(6)]
    last = pltpu.roll(blocks[5], 3 * K, 1)
    moved = [pltpu.roll(blocks[4], (3 - n) * K, 1) for n in range(3)] + [last]
    packed = [jnp.where(lane_in(0, 3 * K), blocks[n], moved[n]) for n in range(4)]
    for b in range(6):
        extra = pltpu.roll(blocks[b], LANES - K + 2 * b, 1)
        last = jnp.where(lane_in(2 * K + 2 * b, 2 * K + 2 * b + 3), extra, last)
    return packed + [last]


def unpack_chunk(packed):
    parts = [packed[SUB * n : SUB * (n + 1)] for n in range(5)]
    four = pltpu.roll(parts[0], K, 1)
    four = jnp.where(lane_in(K, 2 * K), pltpu.roll(parts[1], 2 * K, 1), four)
    four = jnp.where(lane_in(2 * K, 3 * K), pltpu.roll(parts[2], 3 * K, 1), four)
    five = jnp.where(lane_in(0, K), pltpu.roll(parts[3], K, 1), pltpu.roll(parts[4], K, 1))
    sums = jnp.concatenate(parts[:4] + [four, five], axis=0)
    at = [2 * K + 2 * b for b in range(6)]
    gain_sum = jnp.concatenate([parts[4][:, n : n + 1] for n in at], axis=0)
    shift_sum = jnp.concatenate([parts[4][:, n + 1 : n + 2] for n in at], axis=0)
    return sums, gain_sum, shift_sum, parts[4][:1, at[5] + 2 : at[5] + 3]


def back_kernel(
    stat_ref,
    own_ref,
    other_ref,
    par_ref,
    own_field_ref,
    own_conv_ref,
    own_live_ref,
    field_ref,
    conv_ref,
    live_ref,
    out_ref,
    up_ref,
    norm_ref,
):
    tiles = conv_ref.shape[0]
    pairs = out_ref.shape[0]
    per_run = TILE_RUN * LANES // SHARE
    sides = (
        (own_ref, own_field_ref, own_conv_ref, own_live_ref),
        (other_ref, field_ref, conv_ref, live_ref),
    )
    local_frames = added(
        [ref[0, pl.ds(COUNT_AT + u, 1), :] for ref in (own_ref, other_ref) for u in range(UTT)]
    )
    counts = stat_ref[peer_rows(2 * tiles, pairs, tiles), :]
    frames = jnp.sum(counts, axis=0, keepdims=True)
    row = lax.broadcasted_iota(jnp.int32, (SUB, LANES), 0)
    rest = jnp.zeros((K - SUB, LANES), jnp.float32)

    def tile(i):
        means = stat_ref[peer_rows(i, pairs, tiles), :]
        mean_row = jnp.sum(counts * means, axis=0, keepdims=True) / frames
        apart = means - mean_row
        spread = stat_ref[peer_rows(i + tiles, pairs, tiles), :] + counts * apart * apart
        inv_row = lax.rsqrt(jnp.sum(spread, axis=0, keepdims=True) / frames + eps_norm)
        gain_row = par_ref[i, pl.ds(0, 1), :]
        shift_row = par_ref[i, pl.ds(1, 1), :]
        gain_sum = jnp.zeros((SUB, LANES), jnp.float32)
        shift_sum = jnp.zeros((SUB, LANES), jnp.float32)
        for n in range(2 * UTT):
            source_ref, fields_ref, values_ref, mask_ref = sides[n // UTT]
            u = n % UTT
            rows = pl.ds(u * SLOT, SLOT)
            live = mask_ref[rows, :]
            normed = (values_ref[i, rows, :] - mean_row) * inv_row
            norm_out = gain_row * normed + shift_row
            sig = jax.nn.sigmoid(norm_out)
            slope = sig * (1.0 + norm_out * (1.0 - sig))
            upstream = source_ref[i, pl.ds(COT_AT + u * SLOT, SLOT), :] * slope * live
            normed = normed * live
            gain_sum = gain_sum + fold_rows(upstream * normed)
            shift_sum = shift_sum + fold_rows(upstream)
            store_taps(up_ref, fields_ref, i, u, upstream, n == 0)
            store_taps(norm_ref, fields_ref, i, u, normed, n == 0)
        scale = gain_row * inv_row
        extra = jnp.where(row == 0, jnp.sum(gain_sum, axis=0, keepdims=True), local_frames)
        extra = jnp.where(row == 1, jnp.sum(shift_sum, axis=0, keepdims=True), extra)
        live_sum = own_ref[i, pl.ds(LIVE_AT, K), :] + other_ref[i, pl.ds(LIVE_AT, K), :]
        block = jnp.concatenate(
            [load_taps(up_ref) * scale, live_sum * scale, load_taps(norm_ref) * scale, extra, rest],
            axis=0,
        )
        return block.T

    def run(step, carry):
        turned = jnp.concatenate([tile(step * TILE_RUN + n) for n in range(TILE_RUN)], axis=0)
        for j in range(per_run):
            for n, part in enumerate(pack_chunk(turned[j * SHARE : (j + 1) * SHARE])):
                out_ref[step * per_run + j, pl.ds(n * SUB, SUB), :] = part
        return carry

    lax.fori_loop(0, tiles // TILE_RUN, run, 0)


def delta_kernel(sum_ref, drift_ref, drift_norm_ref, out_ref):
    share = SHARE
    channels = drift_ref.shape[2]
    total, gain_sum, shift_sum, frames = unpack_chunk(
        added([sum_ref[p] for p in range(sum_ref.shape[0])])
    )
    live_part = pltpu.roll(total, LANES - K, 1)
    norm_part = pltpu.roll(total, LANES - 2 * K, 1)
    kernel_sum = total - (shift_sum * live_part + gain_sum * norm_part) / frames
    start = lax.axis_index("dp") * share
    first = jnp.minimum(start // LANES, channels // LANES - 2)
    window = pl.ds(pl.multiple_of(first * LANES, LANES), 2 * LANES)
    drift = jnp.concatenate(
        [
            drift_ref[0, :, window].astype(jnp.float32),
            drift_norm_ref[0, :, window].astype(jnp.float32),
            jnp.zeros((LANES - K - 2, 2 * LANES), jnp.float32),
        ],
        axis=0,
    )
    drift = pltpu.roll(drift, lax.rem(2 * LANES - (start - first * LANES), 2 * LANES), 1)
    drift = drift[:, :LANES].T[:share]
    lane = lax.broadcasted_iota(jnp.int32, (share, LANES), 1)
    sums = jnp.where(lane < K, kernel_sum, jnp.where(lane == K, gain_sum, shift_sum))
    delta = (drift + (grad_factor_base / frames) * sums).astype(jnp.bfloat16).astype(jnp.float32)
    weighted = delta * frames
    block = share // 3
    lane = lane[:block]
    packed = jnp.broadcast_to(frames, (block, LANES))
    for b in range(3):
        piece = weighted[b * block : (b + 1) * block]
        moved = pltpu.roll(piece, b * K, 1) if b else piece
        packed = jnp.where((lane >= b * K) & (lane < (b + 1) * K), moved, packed)
        at = 3 * K + 2 * b
        moved = pltpu.roll(piece, at - K, 1)
        packed = jnp.where((lane >= at) & (lane < at + 2), moved, packed)
    for peer in range(out_ref.shape[0]):
        out_ref[peer] = packed


def average_kernel(sum_ref, kernel_ref, norm_ref):
    total = added([sum_ref[p] for p in range(sum_ref.shape[0])])
    block = total.shape[0]
    average = total / total[:, 3 * K + 6 : 3 * K + 7]
    average = jnp.concatenate([average, jnp.zeros((LANES - block, LANES), jnp.float32)], axis=0)
    turned = average.T
    for b in range(3):
        kernel_ref[:, b * block : (b + 1) * block] = turned[b * K : (b + 1) * K, :block]
        norm_ref[:, b * block : (b + 1) * block] = turned[3 * K + 2 * b : 3 * K + 2 * b + 2, :block]


VMEM_SPEC = pl.BlockSpec(memory_space=pltpu.VMEM)
HBM_SPEC = pl.BlockSpec(memory_space=pltpu.HBM)
PARAMS = pltpu.CompilerParams(vmem_limit_bytes=32 * 1024 * 1024)


def cost(flops):
    return pl.CostEstimate(flops=flops, bytes_accessed=0, transcendentals=0)


def gate_stage(frame_count, glu_in, kernel, norm_params, cotangent):
    tiles = cotangent.shape[1] // LANES // 2
    far = [
        pltpu.with_memory_space_constraint(x, pltpu.HBM)
        for x in (frame_count, glu_in, kernel, norm_params, cotangent)
    ]
    return pl.pallas_call(
        gate_kernel,
        out_shape=(
            jax.ShapeDtypeStruct((tiles, PACK_ROWS, LANES), jnp.float32),
            jax.ShapeDtypeStruct((tiles, PACK_ROWS, LANES), jnp.float32),
            jax.ShapeDtypeStruct((tiles, len(PRODUCTS), SUB, LANES), jnp.float32),
            jax.ShapeDtypeStruct((tiles, SUB, LANES), jnp.float32),
        ),
        in_specs=[HBM_SPEC] * 5,
        out_specs=(VMEM_SPEC,) * 4,
        scratch_shapes=[
            pltpu.SMEM((UTT,), jnp.int32),
            pltpu.VMEM(glu_in.shape, glu_in.dtype),
            pltpu.VMEM(kernel.shape, kernel.dtype),
            pltpu.VMEM(norm_params.shape, norm_params.dtype),
            pltpu.VMEM(cotangent.shape, cotangent.dtype),
            pltpu.SemaphoreType.DMA((3,)),
            pltpu.SemaphoreType.DMA((RUNS, 3)),
        ],
        compiler_params=PARAMS,
        name="gate_shares",
    )(*far)


def conv_outputs(tiles):
    return (
        jax.ShapeDtypeStruct((tiles, 4, UTT * PADDED, LANES), jnp.float32),
        jax.ShapeDtypeStruct((tiles, ROWS, LANES), jnp.float32),
        jax.ShapeDtypeStruct((ROWS, LANES), jnp.float32),
    )


def own_conv_stage(own, taps):
    tiles = own.shape[0]
    return pl.pallas_call(
        own_conv_kernel,
        out_shape=(*conv_outputs(tiles), jax.ShapeDtypeStruct((tiles, SUB, LANES), jnp.float32)),
        in_specs=[VMEM_SPEC] * 2,
        out_specs=(VMEM_SPEC,) * 4,
        compiler_params=PARAMS,
        name="own_conv",
    )(own, taps)


def conv_stage(own, other, taps, own_conv, own_live, own_total, peers):
    tiles = own.shape[0]
    return pl.pallas_call(
        conv_kernel,
        out_shape=(
            *conv_outputs(tiles),
            jax.ShapeDtypeStruct((peers * (2 * tiles + 1), LANES), jnp.float32),
        ),
        in_specs=[VMEM_SPEC] * 6,
        out_specs=(VMEM_SPEC,) * 4,
        compiler_params=PARAMS,
        name="conv_stats",
    )(own, other, taps, own_conv, own_live, own_total)


def back_stage(gathered, own, other, norm_rows, own_side, other_side, peers):
    return pl.pallas_call(
        back_kernel,
        out_shape=jax.ShapeDtypeStruct((peers, 5 * SUB, LANES), jnp.float32),
        in_specs=[VMEM_SPEC] * 10,
        out_specs=VMEM_SPEC,
        scratch_shapes=[
            pltpu.VMEM((K * SUB, LANES), jnp.float32),
            pltpu.VMEM((K * SUB, LANES), jnp.float32),
        ],
        compiler_params=PARAMS,
        name="tap_sums",
    )(gathered, own, other, norm_rows, *own_side, *other_side)


def on_device(glu_in, cotangent, frame_count, kernel, norm_params, drift_kernel, drift_norm):
    n_dp = lax.axis_size("dp")
    n_group = lax.axis_size("group")
    pairs = n_dp // 2
    swap = [(i, i ^ 1) for i in range(n_dp)]
    same_core = [[2 * p + core for p in range(pairs)] for core in range(2)]

    own, other, taps, norm_rows = gate_stage(frame_count, glu_in, kernel, norm_params, cotangent)
    other = lax.ppermute(other, "dp", swap)
    *own_side, own_total = own_conv_stage(own, taps)
    *other_side, stats = conv_stage(own, other, taps, own_side[1], own_side[2], own_total, pairs)
    gathered = lax.all_to_all(
        stats.reshape(pairs, 1, -1), "dp", 0, 0, axis_index_groups=same_core
    ).reshape(stats.shape)

    tap_sums = back_stage(gathered, own, other, norm_rows, own_side, other_side, pairs)
    tap_sums = lax.all_to_all(tap_sums, "dp", 0, 0, axis_index_groups=same_core)

    weighted = pl.pallas_call(
        delta_kernel,
        out_shape=jax.ShapeDtypeStruct((n_group, SHARE // 3, LANES), jnp.float32),
        in_specs=[VMEM_SPEC] * 3,
        out_specs=VMEM_SPEC,
        compiler_params=PARAMS,
        name="group_delta",
    )(tap_sums, drift_kernel, drift_norm)
    weighted = lax.all_to_all(weighted, "group", 0, 0)

    return pl.pallas_call(
        average_kernel,
        out_shape=(
            jax.ShapeDtypeStruct((K, SHARE), jnp.float32),
            jax.ShapeDtypeStruct((2, SHARE), jnp.float32),
        ),
        in_specs=[VMEM_SPEC],
        out_specs=(VMEM_SPEC, VMEM_SPEC),
        compiler_params=PARAMS,
        name="group_average",
    )(weighted)


def solution(mesh):
    placed = (
        P(("dp", "group"), None),
        P(("dp", "group"), None),
        P(("dp", "group")),
        P("group", None, None),
        P("group", None, None),
        P("group", None, None),
        P("group", None, None),
    )
    return jax.shard_map(
        on_device,
        mesh=mesh,
        in_specs=placed,
        out_specs=(P(None, "dp"), P(None, "dp")),
        check_vma=False,
    )
```

```python
import functools
import operator

import jax
import jax.numpy as jnp
from jax import lax
from jax.experimental import pallas as pl
from jax.experimental.pallas import tpu as pltpu
from jax.sharding import PartitionSpec as P

K = 32
HALF = K // 2
SUB = 8
LANES = 128
SLOT = 128
UTT = 2
ROWS = UTT * SLOT
PADDED = HALF + SLOT + HALF
SHARE = 48
RUNS = 2
UNROLL = 2
COT_AT = ROWS
LIVE_AT = 2 * ROWS
COUNT_AT = LIVE_AT + K
PACK_ROWS = COUNT_AT + SUB
TILE_RUN = 3

grad_factor_base = 128.0
eps_norm = 1e-05


def lane_tile(i):
    return pl.ds(pl.multiple_of(i * LANES, LANES), LANES)


def peer_rows(row, peers, tiles):
    return pl.ds(row, peers, stride=2 * tiles + 1)


WINDOWS = ((0, 3), (1, 4), (3, 3))


def share_picker(m, core):
    first, count = WINDOWS[m]
    column = lax.broadcasted_iota(jnp.int32, (1, 2 * LANES), 1)
    mine = column < LANES
    at = m * LANES + jnp.where(mine, column, column - LANES)
    shares = added([jnp.where(at >= n * SHARE, 1, 0) for n in range(1, TILE_RUN * LANES // SHARE)])
    source = at + SHARE * (shares + jnp.where(mine, core, 1 - core)) - first * LANES
    row = lax.broadcasted_iota(jnp.int32, (count * LANES, 2 * LANES), 0)
    return jnp.where(row == source, 1.0, 0.0).astype(jnp.bfloat16)


def picked(block, picker):
    return jnp.dot(block, picker, preferred_element_type=jnp.float32)


def live_rows(count):
    return lax.broadcasted_iota(jnp.int32, (SLOT, LANES), 0) < count


def added(terms):
    return functools.reduce(operator.add, terms)


def fold_rows(field):
    return jnp.sum(field.reshape(field.shape[0] // SUB, SUB, LANES), axis=0)


def scan_rows(field, upward):
    row = lax.broadcasted_iota(jnp.int32, field.shape, 0)
    step = 1
    while step < HALF:
        if upward:
            moved = jnp.where(row < HALF - step, pltpu.roll(field, HALF - step, 0), 0.0)
        else:
            moved = jnp.where(row >= step, pltpu.roll(field, step, 0), 0.0)
        field = field + moved
        step *= 2
    return field


PLAIN, NEXT, SECOND, BOTH = range(4)
PRODUCTS = (
    (PLAIN, 3),
    (SECOND, 1),
    (SECOND, 3),
    (NEXT, 2),
    (BOTH, 0),
    (BOTH, 2),
    (NEXT, 3),
    (BOTH, 1),
    (BOTH, 3),
)
COMBOS = ((0, 1, 2, 3), (0, 1), (2, 3), (0, 2), (0,), (2,), (1, 3), (1,), (3,))


def combine(parts):
    low = parts[0] + parts[1]
    high = parts[0] - parts[2]
    return (
        low + (parts[3] + parts[4]),
        low - (parts[6] + parts[7]),
        high + (parts[3] - parts[5]),
        high - (parts[6] - parts[8]),
    )


def fields_at(field_ref, i, row, product):
    kind, block = product
    return [
        field_ref[i, kind, pl.ds(row + SUB * (4 * m + block), SUB), :] for m in range(SLOT // SUB // 4)
    ]


def gate_kernel(
    count_hbm,
    glu_hbm,
    kernel_hbm,
    param_hbm,
    cot_hbm,
    own_ref,
    other_ref,
    taps_ref,
    par_ref,
    count_ref,
    glu_ref,
    kernel_ref,
    param_ref,
    cot_ref,
    small_sems,
    run_sems,
):
    channels = cot_ref.shape[1]
    width = channels // RUNS
    core = lax.rem(lax.axis_index("dp"), 2)
    small = [
        pltpu.make_async_copy(far, close, small_sems.at[n])
        for n, (far, close) in enumerate(
            ((count_hbm, count_ref), (kernel_hbm, kernel_ref), (param_hbm, param_ref))
        )
    ]
    copies = []
    for g in range(RUNS):
        for n, (far, close, at) in enumerate(
            (
                (glu_hbm, glu_ref, g * width),
                (glu_hbm, glu_ref, channels + g * width),
                (cot_hbm, cot_ref, g * width),
            )
        ):
            columns = pl.ds(at, width)
            copies.append(
                pltpu.make_async_copy(far.at[:, columns], close.at[:, columns], run_sems.at[g, n])
            )
    for copy in small + copies:
        copy.start()
    pickers = [share_picker(m, core) for m in range(TILE_RUN)]
    for copy in small:
        copy.wait()
    counts = [count_ref[u] for u in range(UTT)]
    lives = [jnp.where(live_rows(count), 1.0, 0.0) for count in counts]
    row = lax.broadcasted_iota(jnp.int32, (SUB, LANES), 0)
    count_rows = jnp.where(row == 0, counts[0], counts[1]).astype(jnp.float32)
    for g in range(RUNS):
        for copy in copies[3 * g : 3 * g + 3]:
            copy.wait()
        for m, (first, count) in enumerate(WINDOWS):
            t = g * TILE_RUN + m
            start = g * width + first * LANES
            span = count * LANES
            both = pickers[m]
            gated = picked(glu_ref[:, start : start + span], both) * jax.nn.sigmoid(
                picked(glu_ref[:, channels + start : channels + start + span], both)
            )
            cot = picked(cot_ref[:, start : start + span], both)
            small_rows = jnp.concatenate(
                [
                    kernel_ref[0, :, start : start + span].astype(jnp.float32),
                    param_ref[0, :, start : start + span].astype(jnp.float32),
                    jnp.zeros((SUB - 2, span), jnp.float32),
                ],
                axis=0,
            ).astype(jnp.bfloat16)
            small_rows = picked(small_rows, both[:, :LANES])
            rows = [small_rows[SUB * j : SUB * (j + 1)] for j in range(K // SUB)]
            for n, combo in enumerate(COMBOS):
                taps_ref[t, n] = added([rows[j] for j in combo])
            par_ref[t] = small_rows[K:]
            for side, ref in enumerate((own_ref, other_ref)):
                lanes = slice(side * LANES, (side + 1) * LANES)
                heads = []
                tails = []
                sums = []
                for u in range(UTT):
                    part = gated[u * SLOT : (u + 1) * SLOT, lanes] * lives[u]
                    ref[t, pl.ds(u * SLOT, SLOT), :] = part
                    sums.append(fold_rows(part))
                    heads.append(part[:HALF])
                    tails.append(ref[t, pl.ds(u * SLOT + counts[u] - HALF, HALF), :])
                head = added(heads)
                ref[t, pl.ds(COT_AT, ROWS), :] = cot[:, lanes]
                ref[t, pl.ds(LIVE_AT, K), :] = jnp.sum(
                    added(sums), axis=0, keepdims=True
                ) - jnp.concatenate(
                    [scan_rows(added(tails), True), scan_rows(head, False) - head], axis=0
                )
                ref[t, pl.ds(COUNT_AT, SUB), :] = count_rows


def convolve(i, source_ref, taps_ref, live_ref, field_ref, conv_ref):
    edge = jnp.zeros((HALF, LANES), jnp.float32)
    total = jnp.zeros((SUB, LANES), jnp.float32)
    for u in range(UTT):
        base = u * PADDED
        field = source_ref[i, pl.ds(u * SLOT, SLOT), :]
        field = jnp.concatenate([edge, field, edge], axis=0)
        close = field[: PADDED - SUB] - field[SUB:]
        field_ref[i, PLAIN, pl.ds(base, PADDED), :] = field
        field_ref[i, NEXT, pl.ds(base, PADDED - SUB), :] = close
        field_ref[i, SECOND, pl.ds(base, PADDED - 2 * SUB), :] = (
            field[: PADDED - 2 * SUB] - field[2 * SUB :]
        )
        field_ref[i, BOTH, pl.ds(base, PADDED - 3 * SUB), :] = (
            close[: PADDED - 3 * SUB] - close[2 * SUB :]
        )
    for u in range(UTT):
        base = u * PADDED
        sums = [None] * (4 * len(PRODUCTS))
        for first in range(SUB):
            for n, product in enumerate(PRODUCTS):
                tap = taps_ref[i, n, pl.ds(first, 1), :]
                for m, field in enumerate(fields_at(field_ref, i, base + first, product)):
                    term = field * tap
                    sums[4 * n + m] = term if first == 0 else sums[4 * n + m] + term
        for m in range(SLOT // SUB // 4):
            for q, out in enumerate(combine(sums[m::4])):
                at = pl.ds(u * SLOT + SUB * (4 * m + q), SUB)
                conv_ref[i, at, :] = out
                total = total + out * live_ref[at, :]
    return total


def live_masks(source_ref, live_ref):
    position = lax.broadcasted_iota(jnp.int32, (SLOT, LANES), 0).astype(jnp.float32)
    counts = [source_ref[0, pl.ds(COUNT_AT + u, 1), :] for u in range(UTT)]
    for u in range(UTT):
        live_ref[pl.ds(u * SLOT, SLOT), :] = jnp.where(position < counts[u], 1.0, 0.0)
    return added(counts)


def own_conv_kernel(own_ref, taps_ref, field_ref, conv_ref, live_ref, total_ref):
    live_masks(own_ref, live_ref)

    def tile(i, carry):
        total_ref[i] = convolve(i, own_ref, taps_ref, live_ref, field_ref, conv_ref)
        return carry

    lax.fori_loop(0, conv_ref.shape[0], tile, 0, unroll=UNROLL)


def conv_kernel(
    own_ref,
    other_ref,
    taps_ref,
    own_conv_ref,
    own_live_ref,
    own_total_ref,
    field_ref,
    conv_ref,
    live_ref,
    send_ref,
):
    tiles = conv_ref.shape[0]
    peers = send_ref.shape[0] // (2 * tiles + 1)
    own_counts = [own_ref[0, pl.ds(COUNT_AT + u, 1), :] for u in range(UTT)]
    local_frames = live_masks(other_ref, live_ref) + added(own_counts)
    send_ref[peer_rows(2 * tiles, peers, tiles), :] = jnp.broadcast_to(local_frames, (peers, LANES))

    def tile(i, carry):
        total = own_total_ref[i] + convolve(i, other_ref, taps_ref, live_ref, field_ref, conv_ref)
        local_mean = jnp.sum(total, axis=0, keepdims=True) / local_frames
        spread = jnp.zeros((SUB, LANES), jnp.float32)
        for values, live in ((own_conv_ref, own_live_ref), (conv_ref, live_ref)):
            centered = (values[i] - local_mean) * live[...]
            spread = spread + fold_rows(centered * centered)
        spread = jnp.sum(spread, axis=0, keepdims=True)
        send_ref[peer_rows(i, peers, tiles), :] = jnp.broadcast_to(local_mean, (peers, LANES))
        send_ref[peer_rows(i + tiles, peers, tiles), :] = jnp.broadcast_to(spread, (peers, LANES))
        return carry

    lax.fori_loop(0, tiles, tile, 0, unroll=UNROLL)


def store_taps(tap_ref, field_ref, i, u, source, first_part):
    blocks = [source[SUB * q : SUB * (q + 1)] for q in range(SLOT // SUB)]
    mixes = [
        [added([blocks[4 * m + q] for q in combo]) for m in range(SLOT // SUB // 4)]
        for combo in COMBOS
    ]
    for first in range(SUB):
        parts = []
        for mix, product in zip(mixes, PRODUCTS):
            fields = fields_at(field_ref, i, u * PADDED + first, product)
            parts.append(added([x * field for x, field in zip(mix, fields)]))
        for j, out in enumerate(combine(parts)):
            at = pl.ds(SUB * (first + SUB * j), SUB)
            tap_ref[at, :] = out if first_part else tap_ref[at, :] + out


def load_taps(tap_ref):
    return added([tap_ref[pl.ds(row, K, stride=SUB), :] for row in range(SUB)])


def lane_in(low, high):
    lane = lax.broadcasted_iota(jnp.int32, (SUB, LANES), 1)
    return (lane >= low) & (lane < high)


def pack_chunk(chunk):
    blocks = [chunk[SUB * b : SUB * (b + 1)] for b in range(6)]
    last = pltpu.roll(blocks[5], 3 * K, 1)
    moved = [pltpu.roll(blocks[4], (3 - n) * K, 1) for n in range(3)] + [last]
    packed = [jnp.where(lane_in(0, 3 * K), blocks[n], moved[n]) for n in range(4)]
    for b in range(6):
        extra = pltpu.roll(blocks[b], LANES - K + 2 * b, 1)
        last = jnp.where(lane_in(2 * K + 2 * b, 2 * K + 2 * b + 3), extra, last)
    return packed + [last]


def unpack_chunk(packed):
    parts = [packed[SUB * n : SUB * (n + 1)] for n in range(5)]
    four = pltpu.roll(parts[0], K, 1)
    four = jnp.where(lane_in(K, 2 * K), pltpu.roll(parts[1], 2 * K, 1), four)
    four = jnp.where(lane_in(2 * K, 3 * K), pltpu.roll(parts[2], 3 * K, 1), four)
    five = jnp.where(lane_in(0, K), pltpu.roll(parts[3], K, 1), pltpu.roll(parts[4], K, 1))
    sums = jnp.concatenate(parts[:4] + [four, five], axis=0)
    at = [2 * K + 2 * b for b in range(6)]
    gain_sum = jnp.concatenate([parts[4][:, n : n + 1] for n in at], axis=0)
    shift_sum = jnp.concatenate([parts[4][:, n + 1 : n + 2] for n in at], axis=0)
    return sums, gain_sum, shift_sum, parts[4][:1, at[5] + 2 : at[5] + 3]


def back_kernel(
    stat_ref,
    own_ref,
    other_ref,
    par_ref,
    own_field_ref,
    own_conv_ref,
    own_live_ref,
    field_ref,
    conv_ref,
    live_ref,
    out_ref,
    up_ref,
    norm_ref,
):
    tiles = conv_ref.shape[0]
    pairs = out_ref.shape[0]
    per_run = TILE_RUN * LANES // SHARE
    sides = (
        (own_ref, own_field_ref, own_conv_ref, own_live_ref),
        (other_ref, field_ref, conv_ref, live_ref),
    )
    local_frames = added(
        [ref[0, pl.ds(COUNT_AT + u, 1), :] for ref in (own_ref, other_ref) for u in range(UTT)]
    )
    counts = stat_ref[peer_rows(2 * tiles, pairs, tiles), :]
    frames = jnp.sum(counts, axis=0, keepdims=True)
    row = lax.broadcasted_iota(jnp.int32, (SUB, LANES), 0)
    rest = jnp.zeros((K - SUB, LANES), jnp.float32)

    def tile(i):
        means = stat_ref[peer_rows(i, pairs, tiles), :]
        mean_row = jnp.sum(counts * means, axis=0, keepdims=True) / frames
        apart = means - mean_row
        spread = stat_ref[peer_rows(i + tiles, pairs, tiles), :] + counts * apart * apart
        inv_row = lax.rsqrt(jnp.sum(spread, axis=0, keepdims=True) / frames + eps_norm)
        gain_row = par_ref[i, pl.ds(0, 1), :]
        shift_row = par_ref[i, pl.ds(1, 1), :]
        gain_sum = jnp.zeros((SUB, LANES), jnp.float32)
        shift_sum = jnp.zeros((SUB, LANES), jnp.float32)
        for n in range(2 * UTT):
            source_ref, fields_ref, values_ref, mask_ref = sides[n // UTT]
            u = n % UTT
            rows = pl.ds(u * SLOT, SLOT)
            live = mask_ref[rows, :]
            normed = (values_ref[i, rows, :] - mean_row) * inv_row
            norm_out = gain_row * normed + shift_row
            sig = jax.nn.sigmoid(norm_out)
            slope = sig * (1.0 + norm_out * (1.0 - sig))
            upstream = source_ref[i, pl.ds(COT_AT + u * SLOT, SLOT), :] * slope * live
            normed = normed * live
            gain_sum = gain_sum + fold_rows(upstream * normed)
            shift_sum = shift_sum + fold_rows(upstream)
            store_taps(up_ref, fields_ref, i, u, upstream, n == 0)
            store_taps(norm_ref, fields_ref, i, u, normed, n == 0)
        scale = gain_row * inv_row
        extra = jnp.where(row == 0, jnp.sum(gain_sum, axis=0, keepdims=True), local_frames)
        extra = jnp.where(row == 1, jnp.sum(shift_sum, axis=0, keepdims=True), extra)
        live_sum = own_ref[i, pl.ds(LIVE_AT, K), :] + other_ref[i, pl.ds(LIVE_AT, K), :]
        block = jnp.concatenate(
            [load_taps(up_ref) * scale, live_sum * scale, load_taps(norm_ref) * scale, extra, rest],
            axis=0,
        )
        return block.T

    def run(step, carry):
        turned = jnp.concatenate([tile(step * TILE_RUN + n) for n in range(TILE_RUN)], axis=0)
        for j in range(per_run):
            for n, part in enumerate(pack_chunk(turned[j * SHARE : (j + 1) * SHARE])):
                out_ref[step * per_run + j, pl.ds(n * SUB, SUB), :] = part
        return carry

    lax.fori_loop(0, tiles // TILE_RUN, run, 0)


def delta_kernel(sum_ref, drift_ref, drift_norm_ref, out_ref):
    share = SHARE
    channels = drift_ref.shape[2]
    total, gain_sum, shift_sum, frames = unpack_chunk(
        added([sum_ref[p] for p in range(sum_ref.shape[0])])
    )
    live_part = pltpu.roll(total, LANES - K, 1)
    norm_part = pltpu.roll(total, LANES - 2 * K, 1)
    kernel_sum = total - (shift_sum * live_part + gain_sum * norm_part) / frames
    start = lax.axis_index("dp") * share
    first = jnp.minimum(start // LANES, channels // LANES - 2)
    window = pl.ds(pl.multiple_of(first * LANES, LANES), 2 * LANES)
    drift = jnp.concatenate(
        [
            drift_ref[0, :, window].astype(jnp.float32),
            drift_norm_ref[0, :, window].astype(jnp.float32),
            jnp.zeros((LANES - K - 2, 2 * LANES), jnp.float32),
        ],
        axis=0,
    )
    drift = pltpu.roll(drift, lax.rem(2 * LANES - (start - first * LANES), 2 * LANES), 1)
    drift = drift[:, :LANES].T[:share]
    lane = lax.broadcasted_iota(jnp.int32, (share, LANES), 1)
    sums = jnp.where(lane < K, kernel_sum, jnp.where(lane == K, gain_sum, shift_sum))
    delta = (drift + (grad_factor_base / frames) * sums).astype(jnp.bfloat16).astype(jnp.float32)
    weighted = delta * frames
    block = share // 3
    lane = lane[:block]
    packed = jnp.broadcast_to(frames, (block, LANES))
    for b in range(3):
        piece = weighted[b * block : (b + 1) * block]
        moved = pltpu.roll(piece, b * K, 1) if b else piece
        packed = jnp.where((lane >= b * K) & (lane < (b + 1) * K), moved, packed)
        at = 3 * K + 2 * b
        moved = pltpu.roll(piece, at - K, 1)
        packed = jnp.where((lane >= at) & (lane < at + 2), moved, packed)
    for peer in range(out_ref.shape[0]):
        out_ref[peer] = packed


def average_kernel(sum_ref, kernel_ref, norm_ref):
    total = added([sum_ref[p] for p in range(sum_ref.shape[0])])
    block = total.shape[0]
    average = total / total[:, 3 * K + 6 : 3 * K + 7]
    average = jnp.concatenate([average, jnp.zeros((LANES - block, LANES), jnp.float32)], axis=0)
    turned = average.T
    for b in range(3):
        kernel_ref[:, b * block : (b + 1) * block] = turned[b * K : (b + 1) * K, :block]
        norm_ref[:, b * block : (b + 1) * block] = turned[3 * K + 2 * b : 3 * K + 2 * b + 2, :block]


VMEM_SPEC = pl.BlockSpec(memory_space=pltpu.VMEM)
HBM_SPEC = pl.BlockSpec(memory_space=pltpu.HBM)
PARAMS = pltpu.CompilerParams(vmem_limit_bytes=32 * 1024 * 1024)


def cost(flops):
    return pl.CostEstimate(flops=flops, bytes_accessed=0, transcendentals=0)


def gate_stage(frame_count, glu_in, kernel, norm_params, cotangent):
    tiles = cotangent.shape[1] // LANES // 2
    far = [
        pltpu.with_memory_space_constraint(x, pltpu.HBM)
        for x in (frame_count, glu_in, kernel, norm_params, cotangent)
    ]
    return pl.pallas_call(
        gate_kernel,
        out_shape=(
            jax.ShapeDtypeStruct((tiles, PACK_ROWS, LANES), jnp.float32),
            jax.ShapeDtypeStruct((tiles, PACK_ROWS, LANES), jnp.float32),
            jax.ShapeDtypeStruct((tiles, len(PRODUCTS), SUB, LANES), jnp.float32),
            jax.ShapeDtypeStruct((tiles, SUB, LANES), jnp.float32),
        ),
        in_specs=[HBM_SPEC] * 5,
        out_specs=(VMEM_SPEC,) * 4,
        scratch_shapes=[
            pltpu.SMEM((UTT,), jnp.int32),
            pltpu.VMEM(glu_in.shape, glu_in.dtype),
            pltpu.VMEM(kernel.shape, kernel.dtype),
            pltpu.VMEM(norm_params.shape, norm_params.dtype),
            pltpu.VMEM(cotangent.shape, cotangent.dtype),
            pltpu.SemaphoreType.DMA((3,)),
            pltpu.SemaphoreType.DMA((RUNS, 3)),
        ],
        compiler_params=PARAMS,
        name="gate_shares",
    )(*far)


def conv_outputs(tiles):
    return (
        jax.ShapeDtypeStruct((tiles, 4, UTT * PADDED, LANES), jnp.float32),
        jax.ShapeDtypeStruct((tiles, ROWS, LANES), jnp.float32),
        jax.ShapeDtypeStruct((ROWS, LANES), jnp.float32),
    )


def own_conv_stage(own, taps):
    tiles = own.shape[0]
    return pl.pallas_call(
        own_conv_kernel,
        out_shape=(*conv_outputs(tiles), jax.ShapeDtypeStruct((tiles, SUB, LANES), jnp.float32)),
        in_specs=[VMEM_SPEC] * 2,
        out_specs=(VMEM_SPEC,) * 4,
        compiler_params=PARAMS,
        name="own_conv",
    )(own, taps)


def conv_stage(own, other, taps, own_conv, own_live, own_total, peers):
    tiles = own.shape[0]
    return pl.pallas_call(
        conv_kernel,
        out_shape=(
            *conv_outputs(tiles),
            jax.ShapeDtypeStruct((peers * (2 * tiles + 1), LANES), jnp.float32),
        ),
        in_specs=[VMEM_SPEC] * 6,
        out_specs=(VMEM_SPEC,) * 4,
        compiler_params=PARAMS,
        name="conv_stats",
    )(own, other, taps, own_conv, own_live, own_total)


def back_stage(gathered, own, other, norm_rows, own_side, other_side, peers):
    return pl.pallas_call(
        back_kernel,
        out_shape=jax.ShapeDtypeStruct((peers, 5 * SUB, LANES), jnp.float32),
        in_specs=[VMEM_SPEC] * 10,
        out_specs=VMEM_SPEC,
        scratch_shapes=[
            pltpu.VMEM((K * SUB, LANES), jnp.float32),
            pltpu.VMEM((K * SUB, LANES), jnp.float32),
        ],
        compiler_params=PARAMS,
        name="tap_sums",
    )(gathered, own, other, norm_rows, *own_side, *other_side)


def on_device(glu_in, cotangent, frame_count, kernel, norm_params, drift_kernel, drift_norm):
    n_dp = lax.axis_size("dp")
    n_group = lax.axis_size("group")
    pairs = n_dp // 2
    swap = [(i, i ^ 1) for i in range(n_dp)]
    same_core = [[2 * p + core for p in range(pairs)] for core in range(2)]

    own, other, taps, norm_rows = gate_stage(frame_count, glu_in, kernel, norm_params, cotangent)
    other = lax.ppermute(other, "dp", swap)
    *own_side, own_total = own_conv_stage(own, taps)
    *other_side, stats = conv_stage(own, other, taps, own_side[1], own_side[2], own_total, pairs)
    gathered = lax.all_to_all(
        stats.reshape(pairs, 1, -1), "dp", 0, 0, axis_index_groups=same_core
    ).reshape(stats.shape)

    tap_sums = back_stage(gathered, own, other, norm_rows, own_side, other_side, pairs)
    tap_sums = lax.all_to_all(tap_sums, "dp", 0, 0, axis_index_groups=same_core)

    weighted = pl.pallas_call(
        delta_kernel,
        out_shape=jax.ShapeDtypeStruct((n_group, SHARE // 3, LANES), jnp.float32),
        in_specs=[VMEM_SPEC] * 3,
        out_specs=VMEM_SPEC,
        compiler_params=PARAMS,
        name="group_delta",
    )(tap_sums, drift_kernel, drift_norm)
    weighted = lax.all_to_all(weighted, "group", 0, 0)

    return pl.pallas_call(
        average_kernel,
        out_shape=(
            jax.ShapeDtypeStruct((K, SHARE), jnp.float32),
            jax.ShapeDtypeStruct((2, SHARE), jnp.float32),
        ),
        in_specs=[VMEM_SPEC],
        out_specs=(VMEM_SPEC, VMEM_SPEC),
        compiler_params=PARAMS,
        name="group_average",
    )(weighted)


def solution(mesh):
    placed = (
        P(("dp", "group"), None),
        P(("dp", "group"), None),
        P(("dp", "group")),
        P("group", None, None),
        P("group", None, None),
        P("group", None, None),
        P("group", None, None),
    )
    return jax.shard_map(
        on_device,
        mesh=mesh,
        in_specs=placed,
        out_specs=(P(None, "dp"), P(None, "dp")),
        check_vma=False,
    )
```

```python
import functools
import operator

import jax
import jax.numpy as jnp
from jax import lax
from jax.experimental import pallas as pl
from jax.experimental.pallas import tpu as pltpu
from jax.sharding import PartitionSpec as P

K = 32
HALF = K // 2
SUB = 8
LANES = 128
SLOT = 128
UTT = 2
ROWS = UTT * SLOT
PADDED = HALF + SLOT + HALF
SHARE = 48
RUNS = 2
UNROLL = 3
COT_AT = ROWS
LIVE_AT = 2 * ROWS
COUNT_AT = LIVE_AT + K
PACK_ROWS = COUNT_AT + SUB
TILE_RUN = 3

grad_factor_base = 128.0
eps_norm = 1e-05


def lane_tile(i):
    return pl.ds(pl.multiple_of(i * LANES, LANES), LANES)


def peer_rows(row, peers, tiles):
    return pl.ds(row, peers, stride=2 * tiles + 1)


WINDOWS = ((0, 3), (1, 4), (3, 3))


def share_picker(m, core):
    first, count = WINDOWS[m]
    column = lax.broadcasted_iota(jnp.int32, (1, 2 * LANES), 1)
    mine = column < LANES
    at = m * LANES + jnp.where(mine, column, column - LANES)
    shares = added([jnp.where(at >= n * SHARE, 1, 0) for n in range(1, TILE_RUN * LANES // SHARE)])
    source = at + SHARE * (shares + jnp.where(mine, core, 1 - core)) - first * LANES
    row = lax.broadcasted_iota(jnp.int32, (count * LANES, 2 * LANES), 0)
    return jnp.where(row == source, 1.0, 0.0).astype(jnp.bfloat16)


def picked(block, picker):
    return jnp.dot(block, picker, preferred_element_type=jnp.float32)


def live_rows(count):
    return lax.broadcasted_iota(jnp.int32, (SLOT, LANES), 0) < count


def added(terms):
    return functools.reduce(operator.add, terms)


def fold_rows(field):
    return jnp.sum(field.reshape(field.shape[0] // SUB, SUB, LANES), axis=0)


def scan_rows(field, upward):
    row = lax.broadcasted_iota(jnp.int32, field.shape, 0)
    step = 1
    while step < HALF:
        if upward:
            moved = jnp.where(row < HALF - step, pltpu.roll(field, HALF - step, 0), 0.0)
        else:
            moved = jnp.where(row >= step, pltpu.roll(field, step, 0), 0.0)
        field = field + moved
        step *= 2
    return field


PLAIN, NEXT, SECOND, BOTH = range(4)
PRODUCTS = (
    (PLAIN, 3),
    (SECOND, 1),
    (SECOND, 3),
    (NEXT, 2),
    (BOTH, 0),
    (BOTH, 2),
    (NEXT, 3),
    (BOTH, 1),
    (BOTH, 3),
)
COMBOS = ((0, 1, 2, 3), (0, 1), (2, 3), (0, 2), (0,), (2,), (1, 3), (1,), (3,))


def combine(parts):
    low = parts[0] + parts[1]
    high = parts[0] - parts[2]
    return (
        low + (parts[3] + parts[4]),
        low - (parts[6] + parts[7]),
        high + (parts[3] - parts[5]),
        high - (parts[6] - parts[8]),
    )


def fields_at(field_ref, i, row, product):
    kind, block = product
    return [
        field_ref[i, kind, pl.ds(row + SUB * (4 * m + block), SUB), :] for m in range(SLOT // SUB // 4)
    ]


def gate_kernel(
    count_hbm,
    glu_hbm,
    kernel_hbm,
    param_hbm,
    cot_hbm,
    own_ref,
    other_ref,
    taps_ref,
    par_ref,
    count_ref,
    glu_ref,
    kernel_ref,
    param_ref,
    cot_ref,
    small_sems,
    run_sems,
):
    channels = cot_ref.shape[1]
    width = channels // RUNS
    core = lax.rem(lax.axis_index("dp"), 2)
    small = [
        pltpu.make_async_copy(far, close, small_sems.at[n])
        for n, (far, close) in enumerate(
            ((count_hbm, count_ref), (kernel_hbm, kernel_ref), (param_hbm, param_ref))
        )
    ]
    copies = []
    for g in range(RUNS):
        for n, (far, close, at) in enumerate(
            (
                (glu_hbm, glu_ref, g * width),
                (glu_hbm, glu_ref, channels + g * width),
                (cot_hbm, cot_ref, g * width),
            )
        ):
            columns = pl.ds(at, width)
            copies.append(
                pltpu.make_async_copy(far.at[:, columns], close.at[:, columns], run_sems.at[g, n])
            )
    for copy in small + copies:
        copy.start()
    pickers = [share_picker(m, core) for m in range(TILE_RUN)]
    for copy in small:
        copy.wait()
    counts = [count_ref[u] for u in range(UTT)]
    lives = [jnp.where(live_rows(count), 1.0, 0.0) for count in counts]
    row = lax.broadcasted_iota(jnp.int32, (SUB, LANES), 0)
    count_rows = jnp.where(row == 0, counts[0], counts[1]).astype(jnp.float32)
    for g in range(RUNS):
        for copy in copies[3 * g : 3 * g + 3]:
            copy.wait()
        for m, (first, count) in enumerate(WINDOWS):
            t = g * TILE_RUN + m
            start = g * width + first * LANES
            span = count * LANES
            both = pickers[m]
            gated = picked(glu_ref[:, start : start + span], both) * jax.nn.sigmoid(
                picked(glu_ref[:, channels + start : channels + start + span], both)
            )
            cot = picked(cot_ref[:, start : start + span], both)
            small_rows = jnp.concatenate(
                [
                    kernel_ref[0, :, start : start + span].astype(jnp.float32),
                    param_ref[0, :, start : start + span].astype(jnp.float32),
                    jnp.zeros((SUB - 2, span), jnp.float32),
                ],
                axis=0,
            ).astype(jnp.bfloat16)
            small_rows = picked(small_rows, both[:, :LANES])
            rows = [small_rows[SUB * j : SUB * (j + 1)] for j in range(K // SUB)]
            for n, combo in enumerate(COMBOS):
                taps_ref[t, n] = added([rows[j] for j in combo])
            par_ref[t] = small_rows[K:]
            for side, ref in enumerate((own_ref, other_ref)):
                lanes = slice(side * LANES, (side + 1) * LANES)
                heads = []
                tails = []
                sums = []
                for u in range(UTT):
                    part = gated[u * SLOT : (u + 1) * SLOT, lanes] * lives[u]
                    ref[t, pl.ds(u * SLOT, SLOT), :] = part
                    sums.append(fold_rows(part))
                    heads.append(part[:HALF])
                    tails.append(ref[t, pl.ds(u * SLOT + counts[u] - HALF, HALF), :])
                head = added(heads)
                ref[t, pl.ds(COT_AT, ROWS), :] = cot[:, lanes]
                ref[t, pl.ds(LIVE_AT, K), :] = jnp.sum(
                    added(sums), axis=0, keepdims=True
                ) - jnp.concatenate(
                    [scan_rows(added(tails), True), scan_rows(head, False) - head], axis=0
                )
                ref[t, pl.ds(COUNT_AT, SUB), :] = count_rows


def convolve(i, source_ref, taps_ref, live_ref, field_ref, conv_ref):
    edge = jnp.zeros((HALF, LANES), jnp.float32)
    total = jnp.zeros((SUB, LANES), jnp.float32)
    for u in range(UTT):
        base = u * PADDED
        field = source_ref[i, pl.ds(u * SLOT, SLOT), :]
        field = jnp.concatenate([edge, field, edge], axis=0)
        close = field[: PADDED - SUB] - field[SUB:]
        field_ref[i, PLAIN, pl.ds(base, PADDED), :] = field
        field_ref[i, NEXT, pl.ds(base, PADDED - SUB), :] = close
        field_ref[i, SECOND, pl.ds(base, PADDED - 2 * SUB), :] = (
            field[: PADDED - 2 * SUB] - field[2 * SUB :]
        )
        field_ref[i, BOTH, pl.ds(base, PADDED - 3 * SUB), :] = (
            close[: PADDED - 3 * SUB] - close[2 * SUB :]
        )
    for u in range(UTT):
        base = u * PADDED
        sums = [None] * (4 * len(PRODUCTS))
        for first in range(SUB):
            for n, product in enumerate(PRODUCTS):
                tap = taps_ref[i, n, pl.ds(first, 1), :]
                for m, field in enumerate(fields_at(field_ref, i, base + first, product)):
                    term = field * tap
                    sums[4 * n + m] = term if first == 0 else sums[4 * n + m] + term
        for m in range(SLOT // SUB // 4):
            for q, out in enumerate(combine(sums[m::4])):
                at = pl.ds(u * SLOT + SUB * (4 * m + q), SUB)
                conv_ref[i, at, :] = out
                total = total + out * live_ref[at, :]
    return total


def live_masks(source_ref, live_ref):
    position = lax.broadcasted_iota(jnp.int32, (SLOT, LANES), 0).astype(jnp.float32)
    counts = [source_ref[0, pl.ds(COUNT_AT + u, 1), :] for u in range(UTT)]
    for u in range(UTT):
        live_ref[pl.ds(u * SLOT, SLOT), :] = jnp.where(position < counts[u], 1.0, 0.0)
    return added(counts)


def own_conv_kernel(own_ref, taps_ref, field_ref, conv_ref, live_ref, total_ref):
    live_masks(own_ref, live_ref)

    def tile(i, carry):
        total_ref[i] = convolve(i, own_ref, taps_ref, live_ref, field_ref, conv_ref)
        return carry

    lax.fori_loop(0, conv_ref.shape[0], tile, 0, unroll=UNROLL)


def conv_kernel(
    own_ref,
    other_ref,
    taps_ref,
    own_conv_ref,
    own_live_ref,
    own_total_ref,
    field_ref,
    conv_ref,
    live_ref,
    send_ref,
):
    tiles = conv_ref.shape[0]
    peers = send_ref.shape[0] // (2 * tiles + 1)
    own_counts = [own_ref[0, pl.ds(COUNT_AT + u, 1), :] for u in range(UTT)]
    local_frames = live_masks(other_ref, live_ref) + added(own_counts)
    send_ref[peer_rows(2 * tiles, peers, tiles), :] = jnp.broadcast_to(local_frames, (peers, LANES))

    def tile(i, carry):
        total = own_total_ref[i] + convolve(i, other_ref, taps_ref, live_ref, field_ref, conv_ref)
        local_mean = jnp.sum(total, axis=0, keepdims=True) / local_frames
        spread = jnp.zeros((SUB, LANES), jnp.float32)
        for values, live in ((own_conv_ref, own_live_ref), (conv_ref, live_ref)):
            centered = (values[i] - local_mean) * live[...]
            spread = spread + fold_rows(centered * centered)
        spread = jnp.sum(spread, axis=0, keepdims=True)
        send_ref[peer_rows(i, peers, tiles), :] = jnp.broadcast_to(local_mean, (peers, LANES))
        send_ref[peer_rows(i + tiles, peers, tiles), :] = jnp.broadcast_to(spread, (peers, LANES))
        return carry

    lax.fori_loop(0, tiles, tile, 0, unroll=UNROLL)


def store_taps(tap_ref, field_ref, i, u, source, first_part):
    blocks = [source[SUB * q : SUB * (q + 1)] for q in range(SLOT // SUB)]
    mixes = [
        [added([blocks[4 * m + q] for q in combo]) for m in range(SLOT // SUB // 4)]
        for combo in COMBOS
    ]
    for first in range(SUB):
        parts = []
        for mix, product in zip(mixes, PRODUCTS):
            fields = fields_at(field_ref, i, u * PADDED + first, product)
            parts.append(added([x * field for x, field in zip(mix, fields)]))
        for j, out in enumerate(combine(parts)):
            at = pl.ds(SUB * (first + SUB * j), SUB)
            tap_ref[at, :] = out if first_part else tap_ref[at, :] + out


def load_taps(tap_ref):
    return added([tap_ref[pl.ds(row, K, stride=SUB), :] for row in range(SUB)])


def lane_in(low, high):
    lane = lax.broadcasted_iota(jnp.int32, (SUB, LANES), 1)
    return (lane >= low) & (lane < high)


def pack_chunk(chunk):
    blocks = [chunk[SUB * b : SUB * (b + 1)] for b in range(6)]
    last = pltpu.roll(blocks[5], 3 * K, 1)
    moved = [pltpu.roll(blocks[4], (3 - n) * K, 1) for n in range(3)] + [last]
    packed = [jnp.where(lane_in(0, 3 * K), blocks[n], moved[n]) for n in range(4)]
    for b in range(6):
        extra = pltpu.roll(blocks[b], LANES - K + 2 * b, 1)
        last = jnp.where(lane_in(2 * K + 2 * b, 2 * K + 2 * b + 3), extra, last)
    return packed + [last]


def unpack_chunk(packed):
    parts = [packed[SUB * n : SUB * (n + 1)] for n in range(5)]
    four = pltpu.roll(parts[0], K, 1)
    four = jnp.where(lane_in(K, 2 * K), pltpu.roll(parts[1], 2 * K, 1), four)
    four = jnp.where(lane_in(2 * K, 3 * K), pltpu.roll(parts[2], 3 * K, 1), four)
    five = jnp.where(lane_in(0, K), pltpu.roll(parts[3], K, 1), pltpu.roll(parts[4], K, 1))
    sums = jnp.concatenate(parts[:4] + [four, five], axis=0)
    at = [2 * K + 2 * b for b in range(6)]
    gain_sum = jnp.concatenate([parts[4][:, n : n + 1] for n in at], axis=0)
    shift_sum = jnp.concatenate([parts[4][:, n + 1 : n + 2] for n in at], axis=0)
    return sums, gain_sum, shift_sum, parts[4][:1, at[5] + 2 : at[5] + 3]


def back_kernel(
    stat_ref,
    own_ref,
    other_ref,
    par_ref,
    own_field_ref,
    own_conv_ref,
    own_live_ref,
    field_ref,
    conv_ref,
    live_ref,
    out_ref,
    up_ref,
    norm_ref,
):
    tiles = conv_ref.shape[0]
    pairs = out_ref.shape[0]
    per_run = TILE_RUN * LANES // SHARE
    sides = (
        (own_ref, own_field_ref, own_conv_ref, own_live_ref),
        (other_ref, field_ref, conv_ref, live_ref),
    )
    local_frames = added(
        [ref[0, pl.ds(COUNT_AT + u, 1), :] for ref in (own_ref, other_ref) for u in range(UTT)]
    )
    counts = stat_ref[peer_rows(2 * tiles, pairs, tiles), :]
    frames = jnp.sum(counts, axis=0, keepdims=True)
    row = lax.broadcasted_iota(jnp.int32, (SUB, LANES), 0)
    rest = jnp.zeros((K - SUB, LANES), jnp.float32)

    def tile(i):
        means = stat_ref[peer_rows(i, pairs, tiles), :]
        mean_row = jnp.sum(counts * means, axis=0, keepdims=True) / frames
        apart = means - mean_row
        spread = stat_ref[peer_rows(i + tiles, pairs, tiles), :] + counts * apart * apart
        inv_row = lax.rsqrt(jnp.sum(spread, axis=0, keepdims=True) / frames + eps_norm)
        gain_row = par_ref[i, pl.ds(0, 1), :]
        shift_row = par_ref[i, pl.ds(1, 1), :]
        gain_sum = jnp.zeros((SUB, LANES), jnp.float32)
        shift_sum = jnp.zeros((SUB, LANES), jnp.float32)
        for n in range(2 * UTT):
            source_ref, fields_ref, values_ref, mask_ref = sides[n // UTT]
            u = n % UTT
            rows = pl.ds(u * SLOT, SLOT)
            live = mask_ref[rows, :]
            normed = (values_ref[i, rows, :] - mean_row) * inv_row
            norm_out = gain_row * normed + shift_row
            sig = jax.nn.sigmoid(norm_out)
            slope = sig * (1.0 + norm_out * (1.0 - sig))
            upstream = source_ref[i, pl.ds(COT_AT + u * SLOT, SLOT), :] * slope * live
            normed = normed * live
            gain_sum = gain_sum + fold_rows(upstream * normed)
            shift_sum = shift_sum + fold_rows(upstream)
            store_taps(up_ref, fields_ref, i, u, upstream, n == 0)
            store_taps(norm_ref, fields_ref, i, u, normed, n == 0)
        scale = gain_row * inv_row
        extra = jnp.where(row == 0, jnp.sum(gain_sum, axis=0, keepdims=True), local_frames)
        extra = jnp.where(row == 1, jnp.sum(shift_sum, axis=0, keepdims=True), extra)
        live_sum = own_ref[i, pl.ds(LIVE_AT, K), :] + other_ref[i, pl.ds(LIVE_AT, K), :]
        block = jnp.concatenate(
            [load_taps(up_ref) * scale, live_sum * scale, load_taps(norm_ref) * scale, extra, rest],
            axis=0,
        )
        return block.T

    def run(step, carry):
        turned = jnp.concatenate([tile(step * TILE_RUN + n) for n in range(TILE_RUN)], axis=0)
        for j in range(per_run):
            for n, part in enumerate(pack_chunk(turned[j * SHARE : (j + 1) * SHARE])):
                out_ref[step * per_run + j, pl.ds(n * SUB, SUB), :] = part
        return carry

    lax.fori_loop(0, tiles // TILE_RUN, run, 0)


def delta_kernel(sum_ref, drift_ref, drift_norm_ref, out_ref):
    share = SHARE
    channels = drift_ref.shape[2]
    total, gain_sum, shift_sum, frames = unpack_chunk(
        added([sum_ref[p] for p in range(sum_ref.shape[0])])
    )
    live_part = pltpu.roll(total, LANES - K, 1)
    norm_part = pltpu.roll(total, LANES - 2 * K, 1)
    kernel_sum = total - (shift_sum * live_part + gain_sum * norm_part) / frames
    start = lax.axis_index("dp") * share
    first = jnp.minimum(start // LANES, channels // LANES - 2)
    window = pl.ds(pl.multiple_of(first * LANES, LANES), 2 * LANES)
    drift = jnp.concatenate(
        [
            drift_ref[0, :, window].astype(jnp.float32),
            drift_norm_ref[0, :, window].astype(jnp.float32),
            jnp.zeros((LANES - K - 2, 2 * LANES), jnp.float32),
        ],
        axis=0,
    )
    drift = pltpu.roll(drift, lax.rem(2 * LANES - (start - first * LANES), 2 * LANES), 1)
    drift = drift[:, :LANES].T[:share]
    lane = lax.broadcasted_iota(jnp.int32, (share, LANES), 1)
    sums = jnp.where(lane < K, kernel_sum, jnp.where(lane == K, gain_sum, shift_sum))
    delta = (drift + (grad_factor_base / frames) * sums).astype(jnp.bfloat16).astype(jnp.float32)
    weighted = delta * frames
    block = share // 3
    lane = lane[:block]
    packed = jnp.broadcast_to(frames, (block, LANES))
    for b in range(3):
        piece = weighted[b * block : (b + 1) * block]
        moved = pltpu.roll(piece, b * K, 1) if b else piece
        packed = jnp.where((lane >= b * K) & (lane < (b + 1) * K), moved, packed)
        at = 3 * K + 2 * b
        moved = pltpu.roll(piece, at - K, 1)
        packed = jnp.where((lane >= at) & (lane < at + 2), moved, packed)
    for peer in range(out_ref.shape[0]):
        out_ref[peer] = packed


def average_kernel(sum_ref, kernel_ref, norm_ref):
    total = added([sum_ref[p] for p in range(sum_ref.shape[0])])
    block = total.shape[0]
    average = total / total[:, 3 * K + 6 : 3 * K + 7]
    average = jnp.concatenate([average, jnp.zeros((LANES - block, LANES), jnp.float32)], axis=0)
    turned = average.T
    for b in range(3):
        kernel_ref[:, b * block : (b + 1) * block] = turned[b * K : (b + 1) * K, :block]
        norm_ref[:, b * block : (b + 1) * block] = turned[3 * K + 2 * b : 3 * K + 2 * b + 2, :block]


VMEM_SPEC = pl.BlockSpec(memory_space=pltpu.VMEM)
HBM_SPEC = pl.BlockSpec(memory_space=pltpu.HBM)
PARAMS = pltpu.CompilerParams(vmem_limit_bytes=32 * 1024 * 1024)


def cost(flops):
    return pl.CostEstimate(flops=flops, bytes_accessed=0, transcendentals=0)


def gate_stage(frame_count, glu_in, kernel, norm_params, cotangent):
    tiles = cotangent.shape[1] // LANES // 2
    far = [
        pltpu.with_memory_space_constraint(x, pltpu.HBM)
        for x in (frame_count, glu_in, kernel, norm_params, cotangent)
    ]
    return pl.pallas_call(
        gate_kernel,
        out_shape=(
            jax.ShapeDtypeStruct((tiles, PACK_ROWS, LANES), jnp.float32),
            jax.ShapeDtypeStruct((tiles, PACK_ROWS, LANES), jnp.float32),
            jax.ShapeDtypeStruct((tiles, len(PRODUCTS), SUB, LANES), jnp.float32),
            jax.ShapeDtypeStruct((tiles, SUB, LANES), jnp.float32),
        ),
        in_specs=[HBM_SPEC] * 5,
        out_specs=(VMEM_SPEC,) * 4,
        scratch_shapes=[
            pltpu.SMEM((UTT,), jnp.int32),
            pltpu.VMEM(glu_in.shape, glu_in.dtype),
            pltpu.VMEM(kernel.shape, kernel.dtype),
            pltpu.VMEM(norm_params.shape, norm_params.dtype),
            pltpu.VMEM(cotangent.shape, cotangent.dtype),
            pltpu.SemaphoreType.DMA((3,)),
            pltpu.SemaphoreType.DMA((RUNS, 3)),
        ],
        compiler_params=PARAMS,
        name="gate_shares",
    )(*far)


def conv_outputs(tiles):
    return (
        jax.ShapeDtypeStruct((tiles, 4, UTT * PADDED, LANES), jnp.float32),
        jax.ShapeDtypeStruct((tiles, ROWS, LANES), jnp.float32),
        jax.ShapeDtypeStruct((ROWS, LANES), jnp.float32),
    )


def own_conv_stage(own, taps):
    tiles = own.shape[0]
    return pl.pallas_call(
        own_conv_kernel,
        out_shape=(*conv_outputs(tiles), jax.ShapeDtypeStruct((tiles, SUB, LANES), jnp.float32)),
        in_specs=[VMEM_SPEC] * 2,
        out_specs=(VMEM_SPEC,) * 4,
        compiler_params=PARAMS,
        name="own_conv",
    )(own, taps)


def conv_stage(own, other, taps, own_conv, own_live, own_total, peers):
    tiles = own.shape[0]
    return pl.pallas_call(
        conv_kernel,
        out_shape=(
            *conv_outputs(tiles),
            jax.ShapeDtypeStruct((peers * (2 * tiles + 1), LANES), jnp.float32),
        ),
        in_specs=[VMEM_SPEC] * 6,
        out_specs=(VMEM_SPEC,) * 4,
        compiler_params=PARAMS,
        name="conv_stats",
    )(own, other, taps, own_conv, own_live, own_total)


def back_stage(gathered, own, other, norm_rows, own_side, other_side, peers):
    return pl.pallas_call(
        back_kernel,
        out_shape=jax.ShapeDtypeStruct((peers, 5 * SUB, LANES), jnp.float32),
        in_specs=[VMEM_SPEC] * 10,
        out_specs=VMEM_SPEC,
        scratch_shapes=[
            pltpu.VMEM((K * SUB, LANES), jnp.float32),
            pltpu.VMEM((K * SUB, LANES), jnp.float32),
        ],
        compiler_params=PARAMS,
        name="tap_sums",
    )(gathered, own, other, norm_rows, *own_side, *other_side)


def on_device(glu_in, cotangent, frame_count, kernel, norm_params, drift_kernel, drift_norm):
    n_dp = lax.axis_size("dp")
    n_group = lax.axis_size("group")
    pairs = n_dp // 2
    swap = [(i, i ^ 1) for i in range(n_dp)]
    same_core = [[2 * p + core for p in range(pairs)] for core in range(2)]

    own, other, taps, norm_rows = gate_stage(frame_count, glu_in, kernel, norm_params, cotangent)
    other = lax.ppermute(other, "dp", swap)
    *own_side, own_total = own_conv_stage(own, taps)
    *other_side, stats = conv_stage(own, other, taps, own_side[1], own_side[2], own_total, pairs)
    gathered = lax.all_to_all(
        stats.reshape(pairs, 1, -1), "dp", 0, 0, axis_index_groups=same_core
    ).reshape(stats.shape)

    tap_sums = back_stage(gathered, own, other, norm_rows, own_side, other_side, pairs)
    tap_sums = lax.all_to_all(tap_sums, "dp", 0, 0, axis_index_groups=same_core)

    weighted = pl.pallas_call(
        delta_kernel,
        out_shape=jax.ShapeDtypeStruct((n_group, SHARE // 3, LANES), jnp.float32),
        in_specs=[VMEM_SPEC] * 3,
        out_specs=VMEM_SPEC,
        compiler_params=PARAMS,
        name="group_delta",
    )(tap_sums, drift_kernel, drift_norm)
    weighted = lax.all_to_all(weighted, "group", 0, 0)

    return pl.pallas_call(
        average_kernel,
        out_shape=(
            jax.ShapeDtypeStruct((K, SHARE), jnp.float32),
            jax.ShapeDtypeStruct((2, SHARE), jnp.float32),
        ),
        in_specs=[VMEM_SPEC],
        out_specs=(VMEM_SPEC, VMEM_SPEC),
        compiler_params=PARAMS,
        name="group_average",
    )(weighted)


def solution(mesh):
    placed = (
        P(("dp", "group"), None),
        P(("dp", "group"), None),
        P(("dp", "group")),
        P("group", None, None),
        P("group", None, None),
        P("group", None, None),
        P("group", None, None),
    )
    return jax.shard_map(
        on_device,
        mesh=mesh,
        in_specs=placed,
        out_specs=(P(None, "dp"), P(None, "dp")),
        check_vma=False,
    )
```
